32 devices in a mesh: blk: 16 (over z, y, x), aux: 2 (over core).
Axes of the slice: x: 2, y: 2, z: 4, core: 2. Of those that a mesh axis runs over, the one named last changes fastest.
Arguments:
- three_centre: bfloat16 [2048, 4, 4096], P('blk', 'aux'), may hold values from -6 to 6
- occupied_blocks: bfloat16 [128, 64, 64], P('blk'), may hold values from -1.5 to 1.5
- virtual_blocks: bfloat16 [128, 64, 64], P('blk'), may hold values from -1.5 to 1.5
- row_slot: int32 [2048], P('blk'), may hold values from 0 to 7
- col_slot: int32 [2048], P('blk'), may hold values from 0 to 7
- block_owner: int32 [2048, 1], P('blk'), may hold values from 0 to 15; in each aligned block of 128 rows (0 to 127, 128 to 255, ...) at most 16 rows name the same one
Outputs:
- polarizability: float32 [128, 4, 4], P('blk', 'aux')
The draws below stay inside these ranges and needn't reach their ends.
Inputs may be any that keep to these rules, and one draw needn't show every extreme that they name: `block_owner`: among the 128 blocks stored on one index of blk, no owner is named more than 16 times, a bound that some block reaches.
All inputs are finite; a program needn't handle non-finite values.
Results may differ from the reference program's by a relative error of at most 0.0003.
Values may be sent and summed in bfloat16 or wider, within the bound.
No kernel may reach another device: no remote copies, remote signals or barrier semaphores. Data moves between devices by JAX's collectives and lax.ppermute only.
A program may use at most 64 MiB of HBM per device.

```python
import math
import jax
import jax.numpy as jnp
import numpy as np
from jax import lax

BS = 64
GD = 8
NB_DEV = 128
CAP = 16
NG = 128
NB_TOT = 2048
NAUX = 4
N_BLK = 16


def density_draw(key, salt_value):
    base_key = jax.random.fold_in(key, salt_value)
    basis_one, basis_two, spread_key = jax.random.split(base_key, 3)
    left_basis = jnp.linalg.qr(jax.random.normal(basis_one, (NG, BS, BS), jnp.float32))[0]
    right_basis = jnp.linalg.qr(jax.random.normal(basis_two, (NG, BS, BS), jnp.float32))[0]
    spread = jax.random.uniform(spread_key, (NG, BS), jnp.float32)
    low_part = (jnp.arange(BS, dtype=jnp.int32) < BS // 4)[None, :]
    eigen_values = jnp.where(low_part, 0.02 + 0.9 * spread, 0.6 + spread)
    singular = jnp.sqrt(eigen_values)
    scaled = left_basis * singular[:, None, :]
    return jnp.einsum('gij,gkj->gik', scaled, right_basis, precision=lax.Precision.HIGHEST)


def draw_occupied_blocks(key, part):
    return density_draw(key, 11).astype(jnp.bfloat16)


def draw_virtual_blocks(key, part):
    return density_draw(key, 23).astype(jnp.bfloat16)


def set_ends(result, key, least, high):
    spot = [jax.random.randint(jax.random.fold_in(key, axis), (), 0, length) for axis, length in enumerate(result.shape)]
    widest = result.shape.index(max(result.shape))
    neighbour = spot[:widest] + [(spot[widest] + 1) % result.shape[widest]] + spot[widest + 1:]
    return result.at[tuple(spot)].set(least).at[tuple(neighbour)].set(high)


def shard_levels(own_key, extent, cuts, smallest, largest):
    def one(dim, shards_of):
        draws = jax.random.uniform(jax.random.fold_in(jax.random.fold_in(own_key, 6), dim), (shards_of,), jnp.float32, smallest / len(cuts), largest / len(cuts))
        return jnp.repeat(jnp.exp(draws), extent[dim] // shards_of).reshape((-1,) + (1,) * (len(extent) - dim - 1))

    factor_of = one(*cuts[0])
    for cut in cuts[1:]:
        factor_of = factor_of * one(*cut)
    return factor_of


def shared_out(rng, own, number, rows, number_of, top, limit, skew):
    order = jax.random.permutation(rng, number_of)
    crowded, common = load_shares(number_of, rows * top, limit, skew, True), load_shares(number_of, rows * top, limit, skew, False)
    places = jnp.arange(number_of)

    def named(sizes, turn):
        used = int((sizes > 0).sum())
        fixed = max(1, used // 4)
        shifted = fixed + (places - fixed + turn * (used - fixed)) % max(1, number_of - fixed)
        return jnp.zeros((number_of,), jnp.int32).at[order[jnp.where(places < fixed, places, shifted)]].set(jnp.asarray(sizes, jnp.int32))

    sizes = jnp.where(number % 4 == 0, named(crowded, number // 4), named(common, number - number // 4 - 1))
    mixed = jax.random.permutation(jax.random.fold_in(own, 3), number_of)
    donor, sink = mixed[0:number_of // 2 * 2:2], mixed[1:number_of // 2 * 2:2]
    room = jnp.minimum(sizes[donor] - 1, limit - sizes[sink]) // 2
    room = jnp.where((donor == order[0]) | (sink == order[0]) | (sizes[sink] == 0), 0, jnp.maximum(room, 0))
    shifted = jax.random.randint(jax.random.fold_in(own, 4), (number_of // 2,), 0, 1 << 20) % (room + 1)
    sizes = sizes.at[donor].add(-shifted).at[sink].add(shifted)
    labels = jnp.searchsorted(jnp.cumsum(sizes), jnp.arange(rows * top), side="right").astype(jnp.int32)
    grid = labels.reshape(top, rows).T
    grid = grid[jax.random.permutation(jax.random.fold_in(own, 1), rows)]
    turn = jax.random.randint(jax.random.fold_in(own, 2), (rows, 1), 0, top)
    return jnp.take_along_axis(grid, (jnp.arange(top)[None, :] + turn) % top, axis=1)


def load_shares(number_of, total, most, lean, full):
    weights = [(1 << 20) // math.isqrt(grade ** lean) + 1 for grade in range(1, number_of + 1)]
    largest = most if full else min(most, max(-(-total // number_of), total * weights[0] // sum(weights)))
    least = 1 if total - largest >= number_of - 1 else 0
    holding, rest = [largest] + [least] * (number_of - 1), total - largest - least * (number_of - 1)
    while rest > 0:
        candidates = [i for i in range(1, number_of) if holding[i] < largest] or [i for i in range(1, number_of) if holding[i] < most]
        pool, left = sum([weights[i] for i in candidates]), rest
        for i in candidates:
            extra = min(most - holding[i], max(1, left * weights[i] // pool), rest)
            holding[i] = holding[i] + extra
            rest = rest - extra
    return np.array(holding)


def noise(stream_key, dims, width, limit, pieces=(), kind=jnp.bfloat16):
    factor_of = shard_levels(stream_key, dims, pieces, -0.22, 0.18) if pieces else 1.0
    values = jax.random.normal(stream_key, dims, jnp.float32) * width * factor_of
    return jnp.minimum(jnp.maximum(values, -limit), limit).astype(kind)


def setup_inputs(seed: int = 0) -> dict:
    seeds = jax.random.split(jax.random.key(seed), 7)
    three_centre = noise(seeds[0], (NB_TOT, NAUX, BS * BS), 1.0, 6.0, ((0, 16), (1, 2)))
    occupied_blocks = draw_occupied_blocks(jax.random.fold_in(seeds[6], 71), 0)
    virtual_blocks = draw_virtual_blocks(jax.random.fold_in(seeds[6], 71), 0)
    row_slot = set_ends(jax.random.randint(seeds[3], (NB_TOT,), 0, GD), jax.random.fold_in(seeds[3], 1), 0, GD - 1).astype(jnp.int32)
    col_slot = set_ends(jax.random.randint(seeds[4], (NB_TOT,), 0, GD), jax.random.fold_in(seeds[4], 1), 0, GD - 1).astype(jnp.int32)
    block_owner_keys = jax.random.split(jax.random.fold_in(seeds[5], 1), NB_TOT // NB_DEV)
    block_owner_turns = jax.random.permutation(jax.random.fold_in(seeds[5], 3), NB_TOT // NB_DEV)
    block_owner = jax.vmap(lambda own, number: shared_out(jax.random.fold_in(seeds[5], 2), own, number, NB_DEV, N_BLK, 1, CAP, 2))(block_owner_keys, block_owner_turns).reshape((NB_TOT, 1))
    return {"three_centre": three_centre, "occupied_blocks": occupied_blocks, "virtual_blocks": virtual_blocks, "row_slot": row_slot, "col_slot": col_slot, "block_owner": block_owner}


def reference(three_centre, occupied_blocks, virtual_blocks, row_slot, col_slot, block_owner):
    scale = 0.25 / (BS * BS)
    owners = block_owner[:, 0]

    def one_device(chi, index):
        start = (index * NB_DEV).astype(jnp.int32)
        blocks = lax.dynamic_slice_in_dim(three_centre, start, NB_DEV, 0).reshape(NB_DEV, NAUX, BS, BS)
        rows = (index * GD + lax.dynamic_slice_in_dim(row_slot, start, NB_DEV, 0)).astype(jnp.int32)
        cols = (lax.dynamic_slice_in_dim(owners, start, NB_DEV, 0) * GD + lax.dynamic_slice_in_dim(col_slot, start, NB_DEV, 0)).astype(jnp.int32)
        occupied = occupied_blocks[rows].astype(jnp.float32)
        virtual = virtual_blocks[cols].astype(jnp.float32)
        half = jnp.einsum('kpmn,kml->kpln', blocks.astype(jnp.float32), occupied, precision=lax.Precision.HIGHEST).astype(jnp.bfloat16)
        full = jnp.einsum('kpln,kns->kpls', half.astype(jnp.float32), virtual, precision=lax.Precision.HIGHEST).astype(jnp.bfloat16)
        flat = full.reshape(NB_DEV, NAUX, BS * BS).astype(jnp.float32)
        terms = jnp.einsum('kpc,kqc->kpq', flat, flat, precision=lax.Precision.HIGHEST) * scale
        chi = chi.at[cols].add(terms)
        return (chi, None)
    start_chi = jnp.zeros((NG, NAUX, NAUX), jnp.float32)
    chi, _ = lax.scan(one_device, start_chi, jnp.arange(N_BLK, dtype=jnp.int32))
    return chi
```

```python
import functools

import jax
import jax.numpy as jnp
from jax import lax
from jax.experimental import pallas as pl
from jax.experimental.pallas import tpu as pltpu
from jax.sharding import PartitionSpec as P

F32 = jnp.float32
BF16 = jnp.bfloat16
SMEM = pl.BlockSpec(memory_space=pltpu.SMEM)
VMEM = pl.BlockSpec(memory_space=pltpu.VMEM)


def rounds_of(count):
    bits = count.bit_length() - 1
    found = []
    while bits:
        low = (bits - 1) // 2 * 2
        found.append([step << low for step in range(1, 1 << (bits - low))])
        bits = low
    return found


def flip(values, distance, count):
    return lax.ppermute(values, "blk", [(i, i ^ distance) for i in range(count)])


def swap_cores(values):
    return lax.ppermute(values, "aux", [(0, 1), (1, 0)])


def half_kernel(row_slot, blocks_ref, occ_ref, keep_ref, send_ref, expand_ref):
    groups, size, _ = occ_ref.shape
    wide = 2 * size
    core = lax.axis_index("aux")
    row = lax.broadcasted_iota(jnp.int32, (size, wide), 1)
    mu = lax.broadcasted_iota(jnp.int32, (size, wide), 0)
    order = jnp.where(mu == (row % size) // 2 * 2 + row // size, 1.0, 0.0).astype(BF16)
    left = lax.broadcasted_iota(jnp.int32, (wide, wide), 0) // size
    same = left == lax.broadcasted_iota(jnp.int32, (wide, wide), 1) % 2
    for group in range(groups):
        occ = occ_ref[group]
        twice = jnp.concatenate([occ, occ], axis=1)
        spread = lax.dot_general(twice, order, (((0,), (0,)), ((), ())), preferred_element_type=F32)
        expand_ref[group] = jnp.where(same, spread, 0.0).astype(BF16)
    pairs = keep_ref.shape[0]
    near = lax.broadcasted_iota(jnp.int32, (size, wide), 1) < size
    near_out = lax.broadcasted_iota(jnp.int32, (wide, wide), 1) < size

    def one(first, out_ref, index):
        block = 2 * (first + index)
        one_block, two_block = blocks_ref[block], blocks_ref[block + 1]
        one_turned = jnp.concatenate([one_block[:, size:], one_block[:, :size]], axis=1)
        two_turned = jnp.concatenate([two_block[:, size:], two_block[:, :size]], axis=1)
        stacked = jnp.concatenate(
            [jnp.where(near, one_block, two_turned), jnp.where(near, one_turned, two_block)], axis=0
        )
        one_out = jnp.dot(expand_ref[row_slot[block]], stacked, preferred_element_type=F32)
        two_out = jnp.dot(expand_ref[row_slot[block + 1]], stacked, preferred_element_type=F32)
        out_ref[index] = jnp.where(near_out, one_out, two_out).astype(BF16)

    @pl.loop(0, pairs, unroll=4)
    def _(index):
        one((1 - core) * pairs, send_ref, index)

    @pl.loop(0, pairs, unroll=4)
    def _(index):
        one(core * pairs, keep_ref, index)


def chi_kernel(
    count, groups_dev, scale, col_slot, owner, own_ref, other_ref, near_virt, far_virt, out_ref
):
    pairs, wide, _ = own_ref.shape
    size = wide // 2
    core = lax.axis_index("aux")
    me = lax.axis_index("blk")
    half_groups = groups_dev // 2
    groups = count * groups_dev
    lane = lax.broadcasted_iota(jnp.int32, (size, wide), 1)
    low = lane < size
    group_range = lax.broadcasted_iota(jnp.int32, (wide, groups), 1)
    upper = lax.broadcasted_iota(jnp.int32, (wide, groups), 0) < size

    def virt_of(block, keep):
        slot, place = col_slot[block], owner[block] ^ me
        tile = (slot % half_groups) // 2
        is_far = slot // half_groups != core
        found = jnp.where(is_far, far_virt[place, tile], near_virt[place, tile])
        turned = jnp.concatenate([found[:, size:], found[:, :size]], axis=1)
        wanted = jnp.where((slot % 2 == 1) == keep, found, turned)
        mine = (lane >= size) == keep
        return jnp.where(mine, wanted, jnp.zeros_like(wanted))

    def one(index, total):
        block = 2 * (core * pairs + index)
        virt = jnp.concatenate([virt_of(block, False), virt_of(block + 1, True)], axis=0)
        full = []
        for ref in (own_ref, other_ref):
            made = jnp.dot(ref[index], virt, preferred_element_type=F32).astype(BF16).astype(F32)
            full += [made[:size], made[size:]]
        sums = {}
        for p in range(4):
            for q in range(p, 4):
                sums[p, q] = sums[q, p] = jnp.sum(full[p] * full[q], axis=0, keepdims=True)
        rows = [sums[p, q] for p in range(2) for q in range(4)]
        rows += [sums[p, q ^ 2] for p in range(2, 4) for q in range(4)]
        values = jnp.concatenate(rows, axis=0)
        first = values.astype(BF16)
        rest = values - first.astype(F32)
        second = rest.astype(BF16)
        third = (rest - second.astype(F32)).astype(BF16)
        parts = jnp.concatenate([first, second, third], axis=0)
        one_column = owner[block] * groups_dev + col_slot[block]
        two_column = owner[block + 1] * groups_dev + col_slot[block + 1]
        pick = jnp.where(group_range == jnp.where(upper, one_column, two_column), 1.0, 0.0).astype(BF16)
        return total + jnp.dot(parts, pick, preferred_element_type=F32)

    total = lax.fori_loop(0, pairs, one, jnp.zeros((48, groups), F32), unroll=4)
    summed = (total[:16] + total[16:32] + total[32:]) * scale
    for start in range(0, groups, wide):
        square = jnp.concatenate([summed[:, start:start + wide], jnp.zeros((wide - 16, wide), F32)], axis=0)
        out_ref[start:start + wide, :] = square.T


def body(count, three_centre, occupied_blocks, virtual_blocks, row_slot, col_slot, block_owner):
    block_count, aux_local, width = three_centre.shape
    groups_dev, size, _ = occupied_blocks.shape
    scale = 0.25 / (size * size)
    wide = 2 * size
    pairs = block_count // 4
    core = lax.axis_index("aux")
    me = lax.axis_index("blk")
    rounds = rounds_of(count)

    quarter = lax.dynamic_slice_in_dim(virtual_blocks, core * (groups_dev // 2), groups_dev // 2)
    near_virt = jnp.concatenate([quarter[0::2], quarter[1::2]], axis=2)[None]
    blocks = three_centre.reshape(block_count, aux_local, width // wide, wide)
    blocks = blocks.transpose(0, 2, 1, 3).reshape(block_count, size, wide)
    keep, send = pl.pallas_call(
        half_kernel,
        out_shape=[jax.ShapeDtypeStruct((pairs, wide, wide), BF16)] * 2,
        in_specs=[SMEM, VMEM, VMEM],
        out_specs=[VMEM, VMEM],
        scratch_shapes=[pltpu.VMEM((groups_dev, wide, wide), BF16)],
        compiler_params=pltpu.CompilerParams(vmem_limit_bytes=32 * 1024 * 1024),
        cost_estimate=pl.CostEstimate(flops=10**9, bytes_accessed=4 * 1024 * 1024, transcendentals=0),
        name="half",
    )(row_slot, blocks, occupied_blocks)
    other = swap_cores(send)
    for distances in rounds:
        step = distances[0]
        arrived = [near_virt] + [flip(near_virt, distance, count) for distance in distances]
        near_virt = jnp.stack(arrived, axis=1).reshape((-1,) + near_virt.shape[1:])
    far_virt = swap_cores(near_virt)

    partial = pl.pallas_call(
        functools.partial(chi_kernel, count, groups_dev, scale),
        out_shape=jax.ShapeDtypeStruct((count * groups_dev, wide), F32),
        in_specs=[SMEM, SMEM, VMEM, VMEM, VMEM, VMEM],
        out_specs=VMEM,
        compiler_params=pltpu.CompilerParams(vmem_limit_bytes=48 * 1024 * 1024),
        cost_estimate=pl.CostEstimate(flops=10**9, bytes_accessed=4 * 1024 * 1024, transcendentals=0),
        name="chi",
    )(col_slot, block_owner.reshape(block_count), keep, other, near_virt, far_virt)

    partial = partial.reshape(count, groups_dev, wide)
    for distances in rounds:
        parts = len(distances) + 1
        split = partial.reshape(parts, -1, groups_dev, wide)
        mine = me // distances[0] % parts
        partial = lax.dynamic_index_in_dim(split, mine, 0, False)
        for turn, distance in enumerate(distances):
            leaving = lax.dynamic_index_in_dim(split, mine ^ (turn + 1), 0, False)
            partial = partial + flip(leaving, distance, count)
    partial = partial[0]
    theirs = swap_cores(partial[:, :16])
    both = (partial[:, :8] + theirs[:, 8:16]).reshape(groups_dev, 2, 2, 2)
    return jnp.where(core == 0, both, both[:, :, ::-1]).reshape(groups_dev, 2, 4)


def solution(mesh):
    in_specs = (
        P("blk", "aux", None),
        P("blk", None, None),
        P("blk", None, None),
        P("blk"),
        P("blk"),
        P("blk", None),
    )
    out_specs = P("blk", "aux", None)
    return jax.shard_map(
        functools.partial(body, mesh.shape["blk"]),
        mesh=mesh,
        in_specs=in_specs,
        out_specs=out_specs,
        check_vma=False,
    )
```

```python
import functools

import jax
import jax.numpy as jnp
from jax import lax
from jax.experimental import pallas as pl
from jax.experimental.pallas import tpu as pltpu
from jax.sharding import PartitionSpec as P

F32 = jnp.float32
BF16 = jnp.bfloat16
SMEM = pl.BlockSpec(memory_space=pltpu.SMEM)
VMEM = pl.BlockSpec(memory_space=pltpu.VMEM)
HBM = pl.BlockSpec(memory_space=pltpu.HBM)


def rounds_of(count):
    bits = count.bit_length() - 1
    found = []
    while bits:
        low = max(bits - 2, 0)
        found.append([step << low for step in range(1, 1 << (bits - low))])
        bits = low
    return found


def flip(values, distance, count):
    return lax.ppermute(values, "blk", [(i, i ^ distance) for i in range(count)])


def swap_cores(values):
    return lax.ppermute(values, "aux", [(0, 1), (1, 0)])


def split_flip(values, core_zero, core_one, count):
    pairs = [(2 * i + core, 2 * (i ^ distance) + core) for i in range(count) for core, distance in enumerate((core_zero, core_one))]
    return lax.ppermute(values, ("blk", "aux"), pairs)


def expand(occ_ref, expand_ref):
    groups, size, _ = occ_ref.shape
    wide = 2 * size
    column = lax.broadcasted_iota(jnp.int32, (size, wide), 1)
    mu = lax.broadcasted_iota(jnp.int32, (size, wide), 0)
    order = jnp.where(mu == (column % size) // 2 * 2 + column // size, 1.0, 0.0).astype(BF16)
    left = lax.broadcasted_iota(jnp.int32, (wide, wide), 0) // size
    same = left == lax.broadcasted_iota(jnp.int32, (wide, wide), 1) % 2
    for group in range(groups):
        occ = occ_ref[group]
        twice = jnp.concatenate([occ, occ], axis=1)
        spread = lax.dot_general(twice, order, (((0,), (0,)), ((), ())), preferred_element_type=F32)
        expand_ref[group] = jnp.where(same, spread, 0.0).astype(BF16)


def list_blocks(count, groups_dev, slots, owners, list_ref, column_ref):
    total = owners.shape[0]
    quarter = count // 4
    core = lax.axis_index("aux")
    me = lax.axis_index("blk")

    def clear(index, _):
        list_ref[index] = 0
        column_ref[index] = -1
        return 0

    lax.fori_loop(0, total, clear, 0, unroll=8)

    def add(block, found):
        away = owners[block] ^ me
        far = away // quarter
        place = ((far & 1) ^ (1 - core)) * quarter + (away & (quarter - 1))
        list_ref[found] = block
        column_ref[found] = place * groups_dev + slots[block]
        return found + jnp.where(far // 2 == core, 1, 0)

    found = lax.fori_loop(0, total, add, jnp.int32(0), unroll=8)

    @pl.when(found < total)
    def _():
        list_ref[found] = 0
        column_ref[found] = -1

    list_ref[total] = found


def half_kernel(
    count, chunks, rows_ref, slots_ref, owners_ref, own_ref, other_ref, occ_ref,
    own_out, other_out, column_ref, list_ref,
    rows, slots, owners, own, occ, expand_ref, sems,
):
    groups_dev, wide, _ = expand_ref.shape
    size = wide // 2
    total = rows.shape[0]
    copies = [
        pltpu.make_async_copy(source, target, sems.at[index])
        for index, (source, target) in enumerate(
            [(owners_ref, owners), (slots_ref, slots), (rows_ref, rows), (occ_ref, occ), (own_ref, own)]
        )
    ]
    for copy in copies:
        copy.start()
    copies[0].wait()
    copies[1].wait()
    list_blocks(count, groups_dev, slots, owners, list_ref, column_ref)
    copies[3].wait()
    expand(occ, expand_ref)
    copies[2].wait()
    copies[4].wait()
    near = lax.broadcasted_iota(jnp.int32, (size, wide), 1) < size
    near_out = lax.broadcasted_iota(jnp.int32, (wide, wide), 1) < size

    def one(index):
        first, second = list_ref[2 * index], list_ref[2 * index + 1]
        first_row, second_row = rows[first], rows[second]
        for source, out_ref in ((own, own_out), (other_ref, other_out)):
            one_block, two_block = source[first], source[second]
            one_turned = jnp.concatenate([one_block[:, size:], one_block[:, :size]], axis=1)
            two_turned = jnp.concatenate([two_block[:, size:], two_block[:, :size]], axis=1)
            stacked = jnp.concatenate(
                [jnp.where(near, one_block, two_turned), jnp.where(near, one_turned, two_block)], axis=0
            )
            one_made = jnp.dot(expand_ref[first_row], stacked, preferred_element_type=F32)
            two_made = jnp.dot(expand_ref[second_row], stacked, preferred_element_type=F32)
            out_ref[index] = jnp.where(near_out, one_made, two_made).astype(BF16)

    def work(indices, _):
        for index in indices:
            one(index)

    in_chunks(chunks, list_ref[total], work)


def in_chunks(chunks, count, work):
    start = 0
    for length in chunks:
        indices = range(start, start + length)
        if start:
            pl.when(count > 2 * start)(functools.partial(work, indices, False))
        else:
            work(indices, True)
        start += length


def chi_kernel(scale, chunks, list_ref, column_ref, own_ref, other_ref, virt_ref, out_ref, total_ref):
    _, wide, _ = own_ref.shape
    size = wide // 2
    places, _, groups_dev = out_ref.shape
    groups = places * groups_dev
    low = lax.broadcasted_iota(jnp.int32, (size, wide), 1) < size
    low_row = lax.broadcasted_iota(jnp.int32, (16, wide), 1) < size
    group_range = lax.broadcasted_iota(jnp.int32, (16, groups), 1)

    def virt_of(column, part):
        group = jnp.maximum(column, 0)
        found = virt_ref[group // groups_dev, group % groups_dev // 2]
        turned = jnp.concatenate([found[:, size:], found[:, :size]], axis=1)
        placed = jnp.where(group % 2 == part, found, turned)
        return jnp.where(low if part == 0 else ~low, placed, jnp.zeros_like(placed))

    def one(index, total):
        columns = [column_ref[2 * index], column_ref[2 * index + 1]]
        virt = jnp.concatenate([virt_of(column, part) for part, column in enumerate(columns)], axis=0)
        full = []
        for ref in (own_ref, other_ref):
            made = jnp.dot(ref[index], virt, preferred_element_type=F32).astype(BF16).astype(F32)
            full += [made[:size], made[size:]]
        sums = {}
        for p in range(4):
            for q in range(p, 4):
                sums[p, q] = sums[q, p] = jnp.sum(full[p] * full[q], axis=0, keepdims=True)
        rows = [sums[p, q] for p in range(2) for q in range(4)]
        rows += [sums[p, q ^ 2] for p in range(2, 4) for q in range(4)]
        values = jnp.concatenate(rows, axis=0)
        for column, where in zip(columns, (low_row, ~low_row)):
            value = jnp.sum(jnp.where(where, values, 0.0), axis=1, keepdims=True)
            total = total + jnp.where(group_range == column, value, 0.0)
        return total

    def work(indices, is_first):
        total = jnp.zeros((16, groups), F32)
        for index in indices:
            total = one(index, total)
        total_ref[...] = total if is_first else total_ref[...] + total

    in_chunks(chunks, list_ref[list_ref.shape[0] - 1], work)
    summed = total_ref[...] * scale
    for place in range(places):
        out_ref[place] = summed[:, place * groups_dev:(place + 1) * groups_dev]


def body(count, three_centre, occupied_blocks, virtual_blocks, row_slot, col_slot, block_owner):
    block_count, aux_local, width = three_centre.shape
    groups_dev, size, _ = occupied_blocks.shape
    scale = 0.25 / (size * size)
    wide = 2 * size
    pairs = block_count // 4
    core = lax.axis_index("aux")
    rounds = rounds_of(count)
    near, mid, far = rounds[0]

    def by_mu(values):
        found = values.reshape(block_count, aux_local, width // wide, wide)
        return found.transpose(0, 2, 1, 3).reshape(block_count, size, wide)

    def in_hbm(values):
        return pltpu.with_memory_space_constraint(values, pltpu.HBM)

    chunks = (pairs,) + (8,) * (pairs // 8)
    virt = jnp.concatenate([virtual_blocks[0::2], virtual_blocks[1::2]], axis=2)
    other = swap_cores(by_mu(three_centre))
    virt = jnp.stack([split_flip(virt, near, mid, count), split_flip(virt, 0, far, count)])
    virt, rows = lax.optimization_barrier((virt, row_slot))
    half_shape = jax.ShapeDtypeStruct((2 * pairs, wide, wide), BF16)
    integers = pltpu.SMEM((block_count,), jnp.int32)
    own_half, other_half, columns, block_list = pl.pallas_call(
        functools.partial(half_kernel, count, chunks),
        out_shape=[
            half_shape,
            half_shape,
            jax.ShapeDtypeStruct((block_count,), jnp.int32),
            jax.ShapeDtypeStruct((block_count + 1,), jnp.int32),
        ],
        in_specs=[HBM] * 4 + [VMEM, HBM],
        out_specs=[VMEM, VMEM, SMEM, SMEM],
        scratch_shapes=[
            integers,
            integers,
            integers,
            pltpu.VMEM((block_count, size, wide), BF16),
            pltpu.VMEM((groups_dev, size, size), BF16),
            pltpu.VMEM((groups_dev, wide, wide), BF16),
            pltpu.SemaphoreType.DMA((5,)),
        ],
        compiler_params=pltpu.CompilerParams(vmem_limit_bytes=16 * 1024 * 1024),
        cost_estimate=pl.CostEstimate(flops=10**9, bytes_accessed=4 * 1024 * 1024, transcendentals=0),
        name="half",
    )(
        in_hbm(rows), in_hbm(col_slot), in_hbm(block_owner.reshape(block_count)),
        in_hbm(by_mu(three_centre)), other, in_hbm(occupied_blocks),
    )
    for distances in rounds[1:]:
        arrived = [flip(virt, distance, count) for distance in distances]
        if distances is rounds[-1]:
            arrived, own_half = lax.optimization_barrier((arrived, own_half))
        virt = jnp.stack([virt] + arrived, axis=1).reshape((-1,) + virt.shape[1:])

    places = count // 2
    partial = pl.pallas_call(
        functools.partial(chi_kernel, scale, chunks),
        out_shape=jax.ShapeDtypeStruct((places, 16, groups_dev), F32),
        in_specs=[SMEM, SMEM] + [VMEM] * 3,
        out_specs=VMEM,
        scratch_shapes=[pltpu.VMEM((16, places * groups_dev), F32)],
        compiler_params=pltpu.CompilerParams(vmem_limit_bytes=16 * 1024 * 1024),
        cost_estimate=pl.CostEstimate(flops=10**9, bytes_accessed=4 * 1024 * 1024, transcendentals=0),
        name="chi",
    )(block_list, columns, own_half, other_half, virt)

    partial = partial.reshape(2, places // 2, 16, groups_dev)
    partial = split_flip(partial[0], near, mid, count) + split_flip(partial[1], 0, far, count)
    for distances in rounds[1:]:
        split = partial.reshape(len(distances) + 1, -1, 16, groups_dev)
        partial = split[0]
        for turn, distance in enumerate(distances):
            partial = partial + flip(split[turn + 1], distance, count)
    mine = partial[0]
    theirs = swap_cores(mine)
    both = mine[:8] + theirs[8:]
    swapped = both.reshape(2, 2, 2, groups_dev)[:, ::-1].reshape(8, groups_dev)
    return jnp.where(core == 0, both, swapped).reshape(2, 4, groups_dev).transpose(2, 0, 1)


def solution(mesh):
    in_specs = (
        P("blk", "aux", None),
        P("blk", None, None),
        P("blk", None, None),
        P("blk"),
        P("blk"),
        P("blk", None),
    )
    out_specs = P("blk", "aux", None)
    return jax.shard_map(
        functools.partial(body, mesh.shape["blk"]),
        mesh=mesh,
        in_specs=in_specs,
        out_specs=out_specs,
        check_vma=False,
    )
```

```python
import functools

import jax
import jax.numpy as jnp
from jax import lax
from jax.experimental import pallas as pl
from jax.experimental.pallas import tpu as pltpu
from jax.sharding import PartitionSpec as P

F32 = jnp.float32
BF16 = jnp.bfloat16
SMEM = pl.BlockSpec(memory_space=pltpu.SMEM)
VMEM = pl.BlockSpec(memory_space=pltpu.VMEM)
HBM = pl.BlockSpec(memory_space=pltpu.HBM)


def rounds_of(count):
    bits = count.bit_length() - 1
    found = []
    while bits:
        low = max(bits - 2, 0)
        found.append([step << low for step in range(1, 1 << (bits - low))])
        bits = low
    return found


def flip(values, distance, count):
    return lax.ppermute(values, "blk", [(i, i ^ distance) for i in range(count)])


def swap_cores(values):
    return lax.ppermute(values, "aux", [(0, 1), (1, 0)])


def split_flip(values, core_zero, core_one, count):
    pairs = [(2 * i + core, 2 * (i ^ distance) + core) for i in range(count) for core, distance in enumerate((core_zero, core_one))]
    return lax.ppermute(values, ("blk", "aux"), pairs)


def expand(occ_ref, expand_ref):
    groups, size, _ = occ_ref.shape
    wide = 2 * size
    column = lax.broadcasted_iota(jnp.int32, (size, wide), 1)
    mu = lax.broadcasted_iota(jnp.int32, (size, wide), 0)
    order = jnp.where(mu == (column % size) // 2 * 2 + column // size, 1.0, 0.0).astype(BF16)
    left = lax.broadcasted_iota(jnp.int32, (wide, wide), 0) // size
    same = left == lax.broadcasted_iota(jnp.int32, (wide, wide), 1) % 2
    for group in range(groups):
        occ = occ_ref[group]
        twice = jnp.concatenate([occ, occ], axis=1)
        spread = lax.dot_general(twice, order, (((0,), (0,)), ((), ())), preferred_element_type=F32)
        expand_ref[group] = jnp.where(same, spread, 0.0).astype(BF16)


def list_blocks(count, groups_dev, slots, owners, list_ref, column_ref):
    total = owners.shape[0]
    quarter = count // 4
    core = lax.axis_index("aux")
    me = lax.axis_index("blk")

    def clear(index, _):
        list_ref[index] = 0
        column_ref[index] = -1
        return 0

    lax.fori_loop(0, total, clear, 0, unroll=8)

    def add(block, found):
        away = owners[block] ^ me
        far = away // quarter
        place = (1 - (far & 1)) * quarter + (away & (quarter - 1))
        list_ref[found] = block
        column_ref[found] = place * groups_dev + slots[block]
        return found + jnp.where(((far ^ (far // 2)) & 1) == core, 1, 0)

    found = lax.fori_loop(0, total, add, jnp.int32(0), unroll=8)

    @pl.when(found < total)
    def _():
        list_ref[found] = 0
        column_ref[found] = -1

    list_ref[total] = found


def half_kernel(
    count, chunks, rows_ref, slots_ref, owners_ref, own_ref, other_ref, occ_ref,
    own_out, other_out, column_ref, list_ref,
    rows, slots, owners, own, occ, expand_ref, sems,
):
    groups_dev, wide, _ = expand_ref.shape
    size = wide // 2
    total = rows.shape[0]
    copies = [
        pltpu.make_async_copy(source, target, sems.at[index])
        for index, (source, target) in enumerate(
            [(owners_ref, owners), (slots_ref, slots), (rows_ref, rows), (occ_ref, occ), (own_ref, own)]
        )
    ]
    for copy in copies:
        copy.start()
    copies[0].wait()
    copies[1].wait()
    list_blocks(count, groups_dev, slots, owners, list_ref, column_ref)
    copies[3].wait()
    expand(occ, expand_ref)
    copies[2].wait()
    copies[4].wait()
    near = lax.broadcasted_iota(jnp.int32, (size, wide), 1) < size
    near_out = lax.broadcasted_iota(jnp.int32, (wide, wide), 1) < size

    def one(index):
        first, second = list_ref[2 * index], list_ref[2 * index + 1]
        first_row, second_row = rows[first], rows[second]
        stacked = []
        for source in (own, other_ref):
            one_block, two_block = source[first], source[second]
            one_turned = jnp.concatenate([one_block[:, size:], one_block[:, :size]], axis=1)
            two_turned = jnp.concatenate([two_block[:, size:], two_block[:, :size]], axis=1)
            stacked.append(jnp.concatenate(
                [jnp.where(near, one_block, two_turned), jnp.where(near, one_turned, two_block)], axis=0
            ))
        stacked = jnp.concatenate(stacked, axis=1)
        one_made = jnp.dot(expand_ref[first_row], stacked, preferred_element_type=F32)
        two_made = jnp.dot(expand_ref[second_row], stacked, preferred_element_type=F32)
        for part, out_ref in enumerate((own_out, other_out)):
            lanes = slice(part * wide, (part + 1) * wide)
            out_ref[index] = jnp.where(near_out, one_made[:, lanes], two_made[:, lanes]).astype(BF16)

    def work(indices, _):
        for index in indices:
            one(index)

    in_chunks(chunks, list_ref[total], work)


def in_chunks(chunks, count, work):
    start = 0
    for length in chunks:
        indices = range(start, start + length)
        if start:
            pl.when(count > 2 * start)(functools.partial(work, indices, False))
        else:
            work(indices, True)
        start += length


def chi_kernel(scale, chunks, list_ref, column_ref, own_ref, other_ref, virt_ref, out_ref, total_ref):
    _, wide, _ = own_ref.shape
    size = wide // 2
    places, tiles = virt_ref.shape[:2]
    groups_dev = 2 * tiles
    groups = places * groups_dev
    low = lax.broadcasted_iota(jnp.int32, (size, wide), 1) < size
    low_row = lax.broadcasted_iota(jnp.int32, (16, wide), 1) < size
    group_range = lax.broadcasted_iota(jnp.int32, (16, groups), 1)

    def virt_of(column, part):
        group = jnp.maximum(column, 0)
        found = virt_ref[group // groups_dev, group % groups_dev // 2]
        turned = jnp.concatenate([found[:, size:], found[:, :size]], axis=1)
        placed = jnp.where(group % 2 == part, found, turned)
        return jnp.where(low if part == 0 else ~low, placed, jnp.zeros_like(placed))

    def one(index, total):
        columns = [column_ref[2 * index], column_ref[2 * index + 1]]
        virt = jnp.concatenate([virt_of(column, part) for part, column in enumerate(columns)], axis=0)
        full = []
        for ref in (own_ref, other_ref):
            made = jnp.dot(ref[index], virt, preferred_element_type=F32).astype(BF16).astype(F32)
            full += [made[:size], made[size:]]
        sums = {}
        for p in range(4):
            for q in range(p, 4):
                sums[p, q] = sums[q, p] = jnp.sum(full[p] * full[q], axis=0, keepdims=True)
        rows = [sums[p, q] for p in range(2) for q in range(4)]
        rows += [sums[p, q ^ 2] for p in range(2, 4) for q in range(4)]
        values = jnp.concatenate(rows, axis=0)
        for column, where in zip(columns, (low_row, ~low_row)):
            value = jnp.sum(jnp.where(where, values, 0.0), axis=1, keepdims=True)
            total = total + jnp.where(group_range == column, value, 0.0)
        return total

    def work(indices, is_first):
        total = jnp.zeros((16, groups), F32)
        for index in indices:
            total = one(index, total)
        total_ref[...] = total if is_first else total_ref[...] + total

    in_chunks(chunks, list_ref[list_ref.shape[0] - 1], work)
    summed = total_ref[...] * scale
    rows = 8 * groups_dev
    lane = lax.broadcasted_iota(jnp.int32, (8, 2 * rows), 1) // groups_dev % 8
    sublane = lax.broadcasted_iota(jnp.int32, (8, 2 * rows), 0)
    quarter = places // 2
    core = lax.axis_index("aux")
    me = lax.axis_index("blk")
    out_ref[...] = jnp.zeros(out_ref.shape, F32)
    for target in range(2):
        wanted = jnp.where(core == target, summed[:8], summed[8:])
        if target:
            wanted = jnp.concatenate([wanted[2:4], wanted[:2], wanted[6:], wanted[4:6]], axis=0)
        for start in range(0, places, 8):
            piece = wanted[:, start * groups_dev:(start + 8) * groups_dev]
            piece = jnp.concatenate([piece, piece], axis=1)
            turned = jnp.zeros_like(piece)
            for shift in range(8):
                moved = pltpu.roll(pltpu.roll(piece, shift, 0), (2 * rows - groups_dev * shift) % (2 * rows), 1)
                turned = jnp.where(lane == (sublane + 8 - shift) % 8, moved, turned)
            for index in range(8):
                place = start + index
                second = place // quarter
                far = jnp.where(core == 0, 3 - 3 * second, 1 + second)
                owner = me ^ (far * quarter + place % quarter)
                out_ref[pl.ds(2 * owner + target, 1), :] = turned[index:index + 1, :rows]


def body(count, three_centre, occupied_blocks, virtual_blocks, row_slot, col_slot, block_owner):
    block_count, aux_local, width = three_centre.shape
    groups_dev, size, _ = occupied_blocks.shape
    scale = 0.25 / (size * size)
    wide = 2 * size
    pairs = block_count // 4
    core = lax.axis_index("aux")
    rounds = rounds_of(count)
    near, mid, far = rounds[0]

    def by_mu(values):
        found = values.reshape(block_count, aux_local, width // wide, wide)
        return found.transpose(0, 2, 1, 3).reshape(block_count, size, wide)

    def in_hbm(values):
        return pltpu.with_memory_space_constraint(values, pltpu.HBM)

    chunks = (pairs,) + (8,) * (pairs // 8)
    virt = jnp.concatenate([virtual_blocks[0::2], virtual_blocks[1::2]], axis=2)
    other = swap_cores(by_mu(three_centre))
    virt = jnp.stack([split_flip(virt, far, near, count), split_flip(virt, 0, mid, count)])
    virt, rows = lax.optimization_barrier((virt, row_slot))
    half_shape = jax.ShapeDtypeStruct((2 * pairs, wide, wide), BF16)
    integers = pltpu.SMEM((block_count,), jnp.int32)
    own_half, other_half, columns, block_list = pl.pallas_call(
        functools.partial(half_kernel, count, chunks),
        out_shape=[
            half_shape,
            half_shape,
            jax.ShapeDtypeStruct((block_count,), jnp.int32),
            jax.ShapeDtypeStruct((block_count + 1,), jnp.int32),
        ],
        in_specs=[HBM] * 4 + [VMEM, HBM],
        out_specs=[VMEM, VMEM, SMEM, SMEM],
        scratch_shapes=[
            integers,
            integers,
            integers,
            pltpu.VMEM((block_count, size, wide), BF16),
            pltpu.VMEM((groups_dev, size, size), BF16),
            pltpu.VMEM((groups_dev, wide, wide), BF16),
            pltpu.SemaphoreType.DMA((5,)),
        ],
        compiler_params=pltpu.CompilerParams(vmem_limit_bytes=16 * 1024 * 1024),
        cost_estimate=pl.CostEstimate(flops=10**9, bytes_accessed=4 * 1024 * 1024, transcendentals=0),
        name="half",
    )(
        in_hbm(rows), in_hbm(col_slot), in_hbm(block_owner.reshape(block_count)),
        in_hbm(by_mu(three_centre)), other, in_hbm(occupied_blocks),
    )
    for distances in rounds[1:]:
        arrived = [flip(virt, distance, count) for distance in distances]
        if distances is rounds[-1]:
            arrived, own_half = lax.optimization_barrier((arrived, own_half))
        virt = jnp.stack([virt] + arrived, axis=1).reshape((-1,) + virt.shape[1:])

    places = count // 2
    partial = pl.pallas_call(
        functools.partial(chi_kernel, scale, chunks),
        out_shape=jax.ShapeDtypeStruct((2 * count, 8 * groups_dev), F32),
        in_specs=[SMEM, SMEM] + [VMEM] * 3,
        out_specs=VMEM,
        scratch_shapes=[pltpu.VMEM((16, places * groups_dev), F32)],
        compiler_params=pltpu.CompilerParams(vmem_limit_bytes=16 * 1024 * 1024),
        cost_estimate=pl.CostEstimate(flops=10**9, bytes_accessed=4 * 1024 * 1024, transcendentals=0),
        name="chi",
    )(block_list, columns, own_half, other_half, virt)

    arrived = lax.all_to_all(partial, ("blk", "aux"), 0, 0, tiled=True)
    return jnp.sum(arrived, axis=0).reshape(2, 4, groups_dev).transpose(2, 0, 1)


def solution(mesh):
    in_specs = (
        P("blk", "aux", None),
        P("blk", None, None),
        P("blk", None, None),
        P("blk"),
        P("blk"),
        P("blk", None),
    )
    out_specs = P("blk", "aux", None)
    return jax.shard_map(
        functools.partial(body, mesh.shape["blk"]),
        mesh=mesh,
        in_specs=in_specs,
        out_specs=out_specs,
        check_vma=False,
    )
```

```python
import functools

import jax
import jax.numpy as jnp
from jax import lax
from jax.experimental import pallas as pl
from jax.experimental.pallas import tpu as pltpu
from jax.sharding import PartitionSpec as P

F32 = jnp.float32
BF16 = jnp.bfloat16
SMEM = pl.BlockSpec(memory_space=pltpu.SMEM)
VMEM = pl.BlockSpec(memory_space=pltpu.VMEM)
HBM = pl.BlockSpec(memory_space=pltpu.HBM)


def rounds_of(count):
    bits = count.bit_length() - 1
    found = []
    while bits:
        low = max(bits - 2, 0)
        found.append([step << low for step in range(1, 1 << (bits - low))])
        bits = low
    return found


def flip(values, distance, count):
    return lax.ppermute(values, "blk", [(i, i ^ distance) for i in range(count)])


def swap_cores(values):
    return lax.ppermute(values, "aux", [(0, 1), (1, 0)])


def split_flip(values, core_zero, core_one, count):
    pairs = [(2 * i + core, 2 * (i ^ distance) + core) for i in range(count) for core, distance in enumerate((core_zero, core_one))]
    return lax.ppermute(values, ("blk", "aux"), pairs)


def expand(occ_ref, expand_ref):
    groups, size, _ = occ_ref.shape
    wide = 2 * size
    column = lax.broadcasted_iota(jnp.int32, (size, wide), 1)
    mu = lax.broadcasted_iota(jnp.int32, (size, wide), 0)
    order = jnp.where(mu == (column % size) // 2 * 2 + column // size, 1.0, 0.0).astype(BF16)
    left = lax.broadcasted_iota(jnp.int32, (wide, wide), 0) // size
    same = left == lax.broadcasted_iota(jnp.int32, (wide, wide), 1) % 2
    for group in range(groups):
        occ = occ_ref[group]
        twice = jnp.concatenate([occ, occ], axis=1)
        spread = lax.dot_general(twice, order, (((0,), (0,)), ((), ())), preferred_element_type=F32)
        expand_ref[group] = jnp.where(same, spread, 0.0).astype(BF16)


def bits_of(size):
    return size.bit_length() - 1


def list_blocks(count, late_bit, owners, list_ref):
    total = owners.shape[0]
    quarter = count // 4
    core = lax.axis_index("aux")
    me = lax.axis_index("blk") ^ quarter

    def add(block, found):
        early, late = found
        away = owners[block] ^ me
        mine = (((away + quarter) >> (bits_of(quarter) + 1)) & 1) ^ core
        late_here = mine & (away >> late_bit)
        list_ref[jnp.where((away >> late_bit) & 1 == 1, late, early)] = block
        return early + mine - late_here, late + late_here

    early, late = lax.fori_loop(0, total, add, (jnp.int32(0), jnp.int32(total)), unroll=8)
    list_ref[2 * total] = early
    list_ref[2 * total + 1] = late - total


def ready_kernel(
    count, late_bit, rows_ref, slots_ref, owners_ref, occ_ref, expand_ref, list_ref, rows, slots, owners, occ, sems
):
    copies = [
        pltpu.make_async_copy(source, target, sems.at[index])
        for index, (source, target) in enumerate(
            [(owners_ref, owners), (slots_ref, slots), (rows_ref, rows), (occ_ref, occ)]
        )
    ]
    for copy in copies:
        copy.start()

    def clear(index, _):
        list_ref[index] = 0
        return 0

    lax.fori_loop(0, list_ref.shape[0], clear, 0, unroll=43)
    copies[0].wait()
    list_blocks(count, late_bit, owners, list_ref)
    copies[3].wait()
    expand(occ, expand_ref)
    copies[1].wait()
    copies[2].wait()


def half_kernel(chunks, list_ref, rows, own_ref, other_ref, expand_ref, *out_refs):
    total = own_ref.shape[0]
    wide = expand_ref.shape[1]
    size = wide // 2
    near = lax.broadcasted_iota(jnp.int32, (size, wide), 1) < size
    near_out = lax.broadcasted_iota(jnp.int32, (wide, wide), 1) < size

    def one(late, index):
        first, second = [list_ref[late * total + 2 * index + part] for part in range(2)]
        stacked = []
        for source in (own_ref, other_ref):
            one_block, two_block = source[first], source[second]
            one_turned = jnp.concatenate([one_block[:, size:], one_block[:, :size]], axis=1)
            two_turned = jnp.concatenate([two_block[:, size:], two_block[:, :size]], axis=1)
            stacked.append(jnp.concatenate(
                [jnp.where(near, one_block, two_turned), jnp.where(near, one_turned, two_block)], axis=0
            ))
        stacked = jnp.concatenate(stacked, axis=1)
        made = [jnp.dot(expand_ref[rows[block]], stacked, preferred_element_type=F32) for block in (first, second)]
        for part, out_ref in enumerate(out_refs[2 * late:2 * late + 2]):
            lanes = slice(part * wide, (part + 1) * wide)
            out_ref[index] = jnp.where(near_out, made[0][:, lanes], made[1][:, lanes]).astype(BF16)

    for late in range(2):
        def work(indices, _, late=late):
            for index in indices:
                one(late, index)

        in_chunks(chunks, list_ref[2 * total + late], work)


def in_chunks(chunks, count, work):
    start = 0
    for length in chunks:
        indices = range(start, start + length)
        if start:
            pl.when(count > 2 * start)(functools.partial(work, indices, False))
        else:
            work(indices, True)
        start += length


def add_chi(late, chunks, list_ref, slots, owners, own_ref, other_ref, virt_ref, total_ref):
    _, wide, _ = own_ref.shape
    size = wide // 2
    turns, places, tiles = virt_ref.shape[:3]
    groups_dev = 2 * tiles
    groups = total_ref.shape[1]
    all_turns = groups // (places * groups_dev)
    total_blocks = owners.shape[0]
    count = list_ref[2 * total_blocks + late]
    me = lax.axis_index("blk") ^ (places * all_turns // 2)
    low = lax.broadcasted_iota(jnp.int32, (size, wide), 1) < size
    low_row = lax.broadcasted_iota(jnp.int32, (16, wide), 1) < size
    group_range = lax.broadcasted_iota(jnp.int32, (16, groups), 1)

    core = lax.axis_index("aux")

    def virt_of(place, slot, part):
        found = virt_ref[place & (turns - 1), place >> bits_of(all_turns), slot & (tiles - 1)]
        turned = jnp.concatenate([found[:, size:], found[:, :size]], axis=1)
        placed = jnp.where((slot // tiles) ^ core == part, found, turned)
        return jnp.where(low if part == 0 else ~low, placed, jnp.zeros_like(placed))

    def one(index, total):
        blocks = [list_ref[late * total_blocks + 2 * index + part] for part in range(2)]
        found = [(owners[block] ^ me) & (places * all_turns - 1) for block in blocks]
        columns = [place * groups_dev + slots[block] for place, block in zip(found, blocks)]
        virt = jnp.concatenate([virt_of(place, slots[block], part) for part, (place, block) in enumerate(zip(found, blocks))], axis=0)
        full = []
        for ref in (own_ref, other_ref):
            made = jnp.dot(ref[index], virt, preferred_element_type=F32).astype(BF16).astype(F32)
            full += [made[:size], made[size:]]
        sums = {}
        for p in range(4):
            for q in range(p, 4):
                sums[p, q] = sums[q, p] = jnp.sum(full[p] * full[q], axis=0, keepdims=True)
        rows = [sums[p, q] for p in range(2) for q in range(4)]
        rows += [sums[p, q ^ 2] for p in range(2, 4) for q in range(4)]
        values = jnp.concatenate(rows, axis=0)
        for part, where in enumerate((low_row, ~low_row)):
            column = jnp.where(2 * index + part < count, columns[part], -1)
            value = jnp.sum(jnp.where(where, values, 0.0), axis=1, keepdims=True)
            total = total + jnp.where(group_range == column, value, 0.0)
        return total

    def work(indices, is_first):
        total = jnp.zeros((16, groups), F32)
        for index in indices:
            total = one(index, total)
        total_ref[...] = total if is_first and not late else total_ref[...] + total

    in_chunks(chunks, count, work)


def early_kernel(chunks, list_ref, slots, owners, own_ref, other_ref, virt_ref, total_ref):
    add_chi(0, chunks, list_ref, slots, owners, own_ref, other_ref, virt_ref, total_ref)


def late_kernel(scale, chunks, list_ref, slots, owners, own_ref, other_ref, virt_ref, early_ref, out_ref, total_ref):
    total_ref[...] = early_ref[...]
    add_chi(1, chunks, list_ref, slots, owners, own_ref, other_ref, virt_ref, total_ref)
    summed = total_ref[...] * scale
    groups_dev = 2 * virt_ref.shape[2]
    places = summed.shape[1] // groups_dev
    rows = 8 * groups_dev
    lane = lax.broadcasted_iota(jnp.int32, (8, 2 * rows), 1) // groups_dev % 8
    sublane = lax.broadcasted_iota(jnp.int32, (8, 2 * rows), 0)
    quarter = places // 2
    core = lax.axis_index("aux")
    me = lax.axis_index("blk")
    out_ref[...] = jnp.zeros(out_ref.shape, F32)
    for target in range(2):
        wanted = jnp.where(core == target, summed[:8], summed[8:])
        if target:
            wanted = jnp.concatenate([wanted[2:4], wanted[:2], wanted[6:], wanted[4:6]], axis=0)
        for start in range(0, places, 8):
            piece = wanted[:, start * groups_dev:(start + 8) * groups_dev]
            piece = jnp.concatenate([piece, piece], axis=1)
            turned = jnp.zeros_like(piece)
            for shift in range(8):
                moved = pltpu.roll(pltpu.roll(piece, shift, 0), (2 * rows - groups_dev * shift) % (2 * rows), 1)
                turned = jnp.where(lane == (sublane + 8 - shift) % 8, moved, turned)
            for index in range(8):
                place = start + index
                second = place // quarter
                far = jnp.where(core == 0, 3 - 3 * second, 1 + second)
                owner = me ^ (far * quarter + place % quarter)
                out_ref[pl.ds(2 * owner + target, 1), :] = turned[index:index + 1, :rows]


def body(count, three_centre, occupied_blocks, virtual_blocks, row_slot, col_slot, block_owner):
    block_count, aux_local, width = three_centre.shape
    groups_dev, size, _ = occupied_blocks.shape
    scale = 0.25 / (size * size)
    wide = 2 * size
    pairs = block_count // 4
    core = lax.axis_index("aux")
    rounds = rounds_of(count)
    near, mid, far = rounds[0]

    def by_mu(values):
        found = values.reshape(block_count, aux_local, width // wide, wide)
        return found.transpose(0, 2, 1, 3).reshape(block_count, size, wide)

    def in_hbm(values):
        return pltpu.with_memory_space_constraint(values, pltpu.HBM)

    chunks = (5 * pairs // 8,) + (pairs // 8,) * 3 + (pairs // 4,) * 4
    tiles = groups_dev // 2
    left = lax.dynamic_slice_in_dim(virtual_blocks, core * tiles, tiles)
    left, whole = lax.optimization_barrier((left, virtual_blocks))
    virt = jnp.concatenate([left, lax.dynamic_slice_in_dim(whole, (1 - core) * tiles, tiles)], axis=2)
    other = swap_cores(by_mu(three_centre))
    arrived = [split_flip(virt, far, near, count), split_flip(virt, 0, mid, count)]
    integers = pltpu.SMEM((block_count,), jnp.int32)
    options = dict(
        compiler_params=pltpu.CompilerParams(vmem_limit_bytes=16 * 1024 * 1024),
        cost_estimate=pl.CostEstimate(flops=10**9, bytes_accessed=4 * 1024 * 1024, transcendentals=0),
    )
    all_turns = len(rounds[-1]) + 1
    expanded, block_list, rows, slots, owners = pl.pallas_call(
        functools.partial(ready_kernel, count, bits_of(all_turns) - 1),
        out_shape=[
            jax.ShapeDtypeStruct((groups_dev, wide, wide), BF16),
            pltpu.SMEM((2 * block_count + 2,), jnp.int32),
            integers,
            integers,
            integers,
        ],
        in_specs=[HBM] * 4,
        out_specs=[VMEM] + [SMEM] * 4,
        scratch_shapes=[pltpu.VMEM((groups_dev, size, size), BF16), pltpu.SemaphoreType.DMA((4,))],
        name="ready",
        **options,
    )(in_hbm(row_slot), in_hbm(col_slot), in_hbm(block_owner.reshape(block_count)), in_hbm(occupied_blocks))
    arrived, expanded = lax.optimization_barrier((arrived, expanded))
    virt = jnp.stack(arrived)
    half_shape = jax.ShapeDtypeStruct((2 * pairs, wide, wide), BF16)
    halves = pl.pallas_call(
        functools.partial(half_kernel, chunks),
        out_shape=[half_shape] * 4,
        in_specs=[SMEM] * 2 + [VMEM] * 3,
        out_specs=[VMEM] * 4,
        name="half",
        **options,
    )(block_list, rows, by_mu(three_centre), other, expanded)
    for distances in rounds[1:-1]:
        arrived = [flip(virt, distance, count) for distance in distances]
        virt = jnp.stack([virt] + arrived, axis=1).reshape((-1,) + virt.shape[1:])
    arrived = [virt] + [flip(virt, distance, count) for distance in rounds[-1]]
    arrived[:2], halves = lax.optimization_barrier((arrived[:2], halves))
    early = jnp.stack(arrived[:all_turns // 2])
    places = count // 2
    total_shape = (16, places * groups_dev)
    total = pl.pallas_call(
        functools.partial(early_kernel, chunks),
        out_shape=jax.ShapeDtypeStruct(total_shape, F32),
        in_specs=[SMEM] * 3 + [VMEM] * 3,
        out_specs=VMEM,
        name="early",
        **options,
    )(block_list, slots, owners, *halves[:2], early)
    arrived, total = lax.optimization_barrier((arrived[all_turns // 2:], total))
    partial = pl.pallas_call(
        functools.partial(late_kernel, scale, chunks),
        out_shape=jax.ShapeDtypeStruct((2 * count, 8 * groups_dev), F32),
        in_specs=[SMEM] * 3 + [VMEM] * 4,
        out_specs=VMEM,
        scratch_shapes=[pltpu.VMEM(total_shape, F32)],
        name="late",
        **options,
    )(block_list, slots, owners, *halves[2:], jnp.stack(arrived), total)

    arrived = lax.all_to_all(partial, ("blk", "aux"), 0, 0, tiled=True)
    return jnp.sum(arrived, axis=0).reshape(2, 4, groups_dev).transpose(2, 0, 1)


def solution(mesh):
    in_specs = (
        P("blk", "aux", None),
        P("blk", None, None),
        P("blk", None, None),
        P("blk"),
        P("blk"),
        P("blk", None),
    )
    out_specs = P("blk", "aux", None)
    return jax.shard_map(
        functools.partial(body, mesh.shape["blk"]),
        mesh=mesh,
        in_specs=in_specs,
        out_specs=out_specs,
        check_vma=False,
    )
```

```python
import functools

import jax
import jax.numpy as jnp
from jax import lax
from jax.experimental import pallas as pl
from jax.experimental.pallas import tpu as pltpu
from jax.sharding import PartitionSpec as P

F32 = jnp.float32
BF16 = jnp.bfloat16
SMEM = pl.BlockSpec(memory_space=pltpu.SMEM)
VMEM = pl.BlockSpec(memory_space=pltpu.VMEM)
HBM = pl.BlockSpec(memory_space=pltpu.HBM)


def rounds_of(count):
    bits = count.bit_length() - 1
    found = []
    while bits:
        low = max(bits - 2, 0)
        found.append([step << low for step in range(1, 1 << (bits - low))])
        bits = low
    return found


def flip(values, distance, count):
    return lax.ppermute(values, "blk", [(i, i ^ distance) for i in range(count)])


def swap_cores(values):
    return lax.ppermute(values, "aux", [(0, 1), (1, 0)])


def split_flip(values, core_zero, core_one, count):
    pairs = [(2 * i + core, 2 * (i ^ distance) + core) for i in range(count) for core, distance in enumerate((core_zero, core_one))]
    return lax.ppermute(values, ("blk", "aux"), pairs)


def expand(occ_ref, expand_ref):
    groups, size, _ = occ_ref.shape
    wide = 2 * size
    column = lax.broadcasted_iota(jnp.int32, (size, wide), 1)
    mu = lax.broadcasted_iota(jnp.int32, (size, wide), 0)
    order = jnp.where(mu == (column % size) // 2 * 2 + column // size, 1.0, 0.0).astype(BF16)
    left = lax.broadcasted_iota(jnp.int32, (wide, wide), 0) // size
    same = left == lax.broadcasted_iota(jnp.int32, (wide, wide), 1) % 2
    for group in range(groups):
        occ = occ_ref[group]
        twice = jnp.concatenate([occ, occ], axis=1)
        spread = lax.dot_general(twice, order, (((0,), (0,)), ((), ())), preferred_element_type=F32)
        expand_ref[group] = jnp.where(same, spread, 0.0).astype(BF16)


def bits_of(size):
    return size.bit_length() - 1


def list_blocks(count, late_bit, owners, list_ref):
    total = owners.shape[0]
    quarter = count // 4
    core = lax.axis_index("aux")
    me = lax.axis_index("blk") ^ quarter

    def add(block, found):
        early, late = found
        away = owners[block] ^ me
        mine = (away >> (bits_of(quarter) + 1)) ^ (1 - core)
        late_here = mine & (away >> late_bit)
        list_ref[jnp.where((away >> late_bit) & 1 == 1, late, early)] = block
        return early + mine - late_here, late + late_here

    early, late = lax.fori_loop(0, total, add, (jnp.int32(0), jnp.int32(total)), unroll=8)
    list_ref[2 * total] = early
    list_ref[2 * total + 1] = late - total


def ready_kernel(
    count, late_bit, rows_ref, slots_ref, owners_ref, occ_ref, expand_ref, list_ref, rows, slots, owners, occ, sems
):
    copies = [
        pltpu.make_async_copy(source, target, sems.at[index])
        for index, (source, target) in enumerate(
            [(owners_ref, owners), (slots_ref, slots), (rows_ref, rows), (occ_ref, occ)]
        )
    ]
    for copy in copies:
        copy.start()

    def clear(index, _):
        list_ref[index] = 0
        return 0

    lax.fori_loop(0, list_ref.shape[0], clear, 0, unroll=43)
    copies[0].wait()
    list_blocks(count, late_bit, owners, list_ref)
    copies[3].wait()
    expand(occ, expand_ref)
    copies[1].wait()
    copies[2].wait()


def half_kernel(chunks, list_ref, rows, own_ref, other_ref, expand_ref, *out_refs):
    total = own_ref.shape[0]
    wide = expand_ref.shape[1]
    size = wide // 2
    near = lax.broadcasted_iota(jnp.int32, (size, wide), 1) < size
    near_out = lax.broadcasted_iota(jnp.int32, (wide, wide), 1) < size

    def one(late, index):
        first, second = [list_ref[late * total + 2 * index + part] for part in range(2)]
        stacked = []
        for source in (own_ref, other_ref):
            one_block, two_block = source[first], source[second]
            one_turned = jnp.concatenate([one_block[:, size:], one_block[:, :size]], axis=1)
            two_turned = jnp.concatenate([two_block[:, size:], two_block[:, :size]], axis=1)
            stacked.append(jnp.concatenate(
                [jnp.where(near, one_block, two_turned), jnp.where(near, one_turned, two_block)], axis=0
            ))
        stacked = jnp.concatenate(stacked, axis=1)
        made = [jnp.dot(expand_ref[rows[block]], stacked, preferred_element_type=F32) for block in (first, second)]
        for part, out_ref in enumerate(out_refs[2 * late:2 * late + 2]):
            lanes = slice(part * wide, (part + 1) * wide)
            out_ref[index] = jnp.where(near_out, made[0][:, lanes], made[1][:, lanes]).astype(BF16)

    for late in range(2):
        def work(indices, _, late=late):
            for index in indices:
                one(late, index)

        in_chunks(chunks, list_ref[2 * total + late], work)


def in_chunks(chunks, count, work):
    start = 0
    for length in chunks:
        indices = range(start, start + length)
        if start:
            pl.when(count > 2 * start)(functools.partial(work, indices, False))
        else:
            work(indices, True)
        start += length


def add_chi(late, chunks, list_ref, slots, owners, own_ref, other_ref, virt_ref, total_ref):
    _, wide, _ = own_ref.shape
    size = wide // 2
    turns, places, tiles = virt_ref.shape[:3]
    groups_dev = 2 * tiles
    groups = total_ref.shape[1]
    all_turns = groups // (places * groups_dev)
    total_blocks = owners.shape[0]
    count = list_ref[2 * total_blocks + late]
    me = lax.axis_index("blk") ^ (places * all_turns // 2)
    low = lax.broadcasted_iota(jnp.int32, (size, wide), 1) < size
    low_row = lax.broadcasted_iota(jnp.int32, (16, wide), 1) < size
    group_range = lax.broadcasted_iota(jnp.int32, (16, groups), 1)

    core = lax.axis_index("aux")

    def virt_of(place, slot, part):
        found = virt_ref[place & (turns - 1), place >> bits_of(all_turns), slot & (tiles - 1)]
        turned = jnp.concatenate([found[:, size:], found[:, :size]], axis=1)
        placed = jnp.where((slot // tiles) ^ core == part, found, turned)
        return jnp.where(low if part == 0 else ~low, placed, jnp.zeros_like(placed))

    def one(index, total):
        blocks = [list_ref[late * total_blocks + 2 * index + part] for part in range(2)]
        found = [(owners[block] ^ me) & (places * all_turns - 1) for block in blocks]
        columns = [place * groups_dev + slots[block] for place, block in zip(found, blocks)]
        virt = jnp.concatenate([virt_of(place, slots[block], part) for part, (place, block) in enumerate(zip(found, blocks))], axis=0)
        full = []
        for ref in (own_ref, other_ref):
            made = jnp.dot(ref[index], virt, preferred_element_type=F32).astype(BF16).astype(F32)
            full += [made[:size], made[size:]]
        sums = {}
        for p in range(4):
            for q in range(p, 4):
                sums[p, q] = sums[q, p] = jnp.sum(full[p] * full[q], axis=0, keepdims=True)
        rows = [sums[p, q] for p in range(2) for q in range(4)]
        rows += [sums[p, q ^ 2] for p in range(2, 4) for q in range(4)]
        values = jnp.concatenate(rows, axis=0)
        for part, where in enumerate((low_row, ~low_row)):
            column = jnp.where(2 * index + part < count, columns[part], -1)
            value = jnp.sum(jnp.where(where, values, 0.0), axis=1, keepdims=True)
            total = total + jnp.where(group_range == column, value, 0.0)
        return total

    def work(indices, is_first):
        total = jnp.zeros((16, groups), F32)
        for index in indices:
            total = one(index, total)
        total_ref[...] = total if is_first and not late else total_ref[...] + total

    in_chunks(chunks, count, work)


def early_kernel(chunks, list_ref, slots, owners, own_ref, other_ref, virt_ref, total_ref):
    add_chi(0, chunks, list_ref, slots, owners, own_ref, other_ref, virt_ref, total_ref)


def late_kernel(scale, chunks, list_ref, slots, owners, own_ref, other_ref, virt_ref, early_ref, out_ref, total_ref):
    total_ref[...] = early_ref[...]
    add_chi(1, chunks, list_ref, slots, owners, own_ref, other_ref, virt_ref, total_ref)
    summed = total_ref[...] * scale
    groups_dev = 2 * virt_ref.shape[2]
    places = summed.shape[1] // groups_dev
    rows = 8 * groups_dev
    lane = lax.broadcasted_iota(jnp.int32, (8, 2 * rows), 1) // groups_dev % 8
    sublane = lax.broadcasted_iota(jnp.int32, (8, 2 * rows), 0)
    quarter = places // 2
    core = lax.axis_index("aux")
    me = lax.axis_index("blk")
    out_ref[...] = jnp.zeros(out_ref.shape, F32)
    for target in range(2):
        wanted = jnp.where(core == target, summed[:8], summed[8:])
        if target:
            wanted = jnp.concatenate([wanted[2:4], wanted[:2], wanted[6:], wanted[4:6]], axis=0)
        for start in range(0, places, 8):
            piece = wanted[:, start * groups_dev:(start + 8) * groups_dev]
            piece = jnp.concatenate([piece, piece], axis=1)
            turned = jnp.zeros_like(piece)
            for shift in range(8):
                moved = pltpu.roll(pltpu.roll(piece, shift, 0), (2 * rows - groups_dev * shift) % (2 * rows), 1)
                turned = jnp.where(lane == (sublane + 8 - shift) % 8, moved, turned)
            for index in range(8):
                place = start + index
                second = place // quarter
                far = 2 * core + 1 - second
                owner = me ^ (far * quarter + place % quarter)
                out_ref[pl.ds(2 * owner + target, 1), :] = turned[index:index + 1, :rows]


def body(count, three_centre, occupied_blocks, virtual_blocks, row_slot, col_slot, block_owner):
    block_count, aux_local, width = three_centre.shape
    groups_dev, size, _ = occupied_blocks.shape
    scale = 0.25 / (size * size)
    wide = 2 * size
    pairs = block_count // 4
    core = lax.axis_index("aux")
    rounds = rounds_of(count)
    near, mid, far = rounds[0]

    def by_mu(values):
        found = values.reshape(block_count, aux_local, width // wide, wide)
        return found.transpose(0, 2, 1, 3).reshape(block_count, size, wide)

    def in_hbm(values):
        return pltpu.with_memory_space_constraint(values, pltpu.HBM)

    chunks = (5 * pairs // 8,) + (pairs // 8,) * 3 + (pairs // 4,) * 4
    tiles = groups_dev // 2
    left = lax.dynamic_slice_in_dim(virtual_blocks, core * tiles, tiles)
    left, whole = lax.optimization_barrier((left, virtual_blocks))
    virt = jnp.concatenate([left, lax.dynamic_slice_in_dim(whole, (1 - core) * tiles, tiles)], axis=2)
    other = swap_cores(by_mu(three_centre))
    arrived = [split_flip(virt, near, far, count), split_flip(virt, 0, mid, count)]
    integers = pltpu.SMEM((block_count,), jnp.int32)
    options = dict(
        compiler_params=pltpu.CompilerParams(vmem_limit_bytes=16 * 1024 * 1024),
        cost_estimate=pl.CostEstimate(flops=10**9, bytes_accessed=4 * 1024 * 1024, transcendentals=0),
    )
    all_turns = len(rounds[-1]) + 1
    expanded, block_list, rows, slots, owners = pl.pallas_call(
        functools.partial(ready_kernel, count, bits_of(all_turns) - 1),
        out_shape=[
            jax.ShapeDtypeStruct((groups_dev, wide, wide), BF16),
            pltpu.SMEM((2 * block_count + 2,), jnp.int32),
            integers,
            integers,
            integers,
        ],
        in_specs=[HBM] * 4,
        out_specs=[VMEM] + [SMEM] * 4,
        scratch_shapes=[pltpu.VMEM((groups_dev, size, size), BF16), pltpu.SemaphoreType.DMA((4,))],
        name="ready",
        **options,
    )(in_hbm(row_slot), in_hbm(col_slot), in_hbm(block_owner.reshape(block_count)), in_hbm(occupied_blocks))
    arrived, expanded = lax.optimization_barrier((arrived, expanded))
    virt = jnp.stack(arrived)
    half_shape = jax.ShapeDtypeStruct((2 * pairs, wide, wide), BF16)
    halves = pl.pallas_call(
        functools.partial(half_kernel, chunks),
        out_shape=[half_shape] * 4,
        in_specs=[SMEM] * 2 + [VMEM] * 3,
        out_specs=[VMEM] * 4,
        name="half",
        **options,
    )(block_list, rows, by_mu(three_centre), other, expanded)
    for distances in rounds[1:-1]:
        arrived = [flip(virt, distance, count) for distance in distances]
        virt = jnp.stack([virt] + arrived, axis=1).reshape((-1,) + virt.shape[1:])
    arrived = [virt] + [flip(virt, distance, count) for distance in rounds[-1]]
    arrived[:2], halves = lax.optimization_barrier((arrived[:2], halves))
    early = jnp.stack(arrived[:all_turns // 2])
    places = count // 2
    total_shape = (16, places * groups_dev)
    total = pl.pallas_call(
        functools.partial(early_kernel, chunks),
        out_shape=jax.ShapeDtypeStruct(total_shape, F32),
        in_specs=[SMEM] * 3 + [VMEM] * 3,
        out_specs=VMEM,
        name="early",
        **options,
    )(block_list, slots, owners, *halves[:2], early)
    arrived, total = lax.optimization_barrier((arrived[all_turns // 2:], total))
    partial = pl.pallas_call(
        functools.partial(late_kernel, scale, chunks),
        out_shape=jax.ShapeDtypeStruct((2 * count, 8 * groups_dev), F32),
        in_specs=[SMEM] * 3 + [VMEM] * 4,
        out_specs=VMEM,
        scratch_shapes=[pltpu.VMEM(total_shape, F32)],
        name="late",
        **options,
    )(block_list, slots, owners, *halves[2:], jnp.stack(arrived), total)

    arrived = lax.all_to_all(partial, ("blk", "aux"), 0, 0, tiled=True)
    return jnp.sum(arrived, axis=0).reshape(2, 4, groups_dev).transpose(2, 0, 1)


def solution(mesh):
    in_specs = (
        P("blk", "aux", None),
        P("blk", None, None),
        P("blk", None, None),
        P("blk"),
        P("blk"),
        P("blk", None),
    )
    out_specs = P("blk", "aux", None)
    return jax.shard_map(
        functools.partial(body, mesh.shape["blk"]),
        mesh=mesh,
        in_specs=in_specs,
        out_specs=out_specs,
        check_vma=False,
    )
```

```python
import functools

import jax
import jax.numpy as jnp
from jax import lax
from jax.experimental import pallas as pl
from jax.experimental.pallas import tpu as pltpu
from jax.sharding import PartitionSpec as P

F32 = jnp.float32
BF16 = jnp.bfloat16
SMEM = pl.BlockSpec(memory_space=pltpu.SMEM)
VMEM = pl.BlockSpec(memory_space=pltpu.VMEM)
HBM = pl.BlockSpec(memory_space=pltpu.HBM)


def rounds_of(count):
    bits = count.bit_length() - 1
    found = []
    while bits:
        low = max(bits - 2, 0)
        found.append([step << low for step in range(1, 1 << (bits - low))])
        bits = low
    return found


def flip(values, distance, count):
    return lax.ppermute(values, "blk", [(i, i ^ distance) for i in range(count)])


def swap_cores(values):
    return lax.ppermute(values, "aux", [(0, 1), (1, 0)])


def split_flip(values, core_zero, core_one, count):
    pairs = [(2 * i + core, 2 * (i ^ distance) + core) for i in range(count) for core, distance in enumerate((core_zero, core_one))]
    return lax.ppermute(values, ("blk", "aux"), pairs)


def expand(occ_ref, expand_ref):
    groups, size, _ = occ_ref.shape
    wide = 2 * size
    column = lax.broadcasted_iota(jnp.int32, (size, wide), 1)
    mu = lax.broadcasted_iota(jnp.int32, (size, wide), 0)
    order = jnp.where(mu == (column % size) // 2 * 2 + column // size, 1.0, 0.0).astype(BF16)
    left = lax.broadcasted_iota(jnp.int32, (wide, wide), 0) // size
    same = left == lax.broadcasted_iota(jnp.int32, (wide, wide), 1) % 2
    for group in range(groups):
        occ = occ_ref[group]
        twice = jnp.concatenate([occ, occ], axis=1)
        spread = lax.dot_general(twice, order, (((0,), (0,)), ((), ())), preferred_element_type=F32)
        expand_ref[group] = jnp.where(same, spread, 0.0).astype(BF16)


def bits_of(size):
    return size.bit_length() - 1


def list_blocks(count, late_bit, owners, list_ref):
    total = owners.shape[0]
    quarter = count // 4
    core = lax.axis_index("aux")
    me = lax.axis_index("blk") ^ quarter

    def add(block, found):
        early, late = found
        away = owners[block] ^ me
        mine = (away >> (bits_of(quarter) + 1)) ^ (1 - core)
        late_here = mine & (away >> late_bit)
        list_ref[jnp.where((away >> late_bit) & 1 == 1, late, early)] = block
        return early + mine - late_here, late + late_here

    early, late = lax.fori_loop(0, total, add, (jnp.int32(0), jnp.int32(total)), unroll=8)
    list_ref[2 * total] = early
    list_ref[2 * total + 1] = late - total


def ready_kernel(
    count, late_bit, rows_ref, slots_ref, owners_ref, occ_ref, expand_ref, list_ref, rows, slots, owners, occ, sems
):
    copies = [
        pltpu.make_async_copy(source, target, sems.at[index])
        for index, (source, target) in enumerate(
            [(owners_ref, owners), (slots_ref, slots), (rows_ref, rows), (occ_ref, occ)]
        )
    ]
    for copy in copies:
        copy.start()

    def clear(index, _):
        list_ref[index] = 0
        return 0

    lax.fori_loop(0, list_ref.shape[0], clear, 0, unroll=43)
    copies[0].wait()
    list_blocks(count, late_bit, owners, list_ref)
    copies[3].wait()
    expand(occ, expand_ref)
    copies[1].wait()
    copies[2].wait()


def half_kernel(chunks, list_ref, rows, own_ref, other_ref, expand_ref, *out_refs):
    total = own_ref.shape[0]
    wide = expand_ref.shape[1]
    size = wide // 2
    near = lax.broadcasted_iota(jnp.int32, (size, wide), 1) < size
    near_out = lax.broadcasted_iota(jnp.int32, (wide, wide), 1) < size

    def one(late, index):
        first, second = [list_ref[late * total + 2 * index + part] for part in range(2)]
        stacked = []
        for source in (own_ref, other_ref):
            one_block, two_block = source[first], source[second]
            one_turned = jnp.concatenate([one_block[:, size:], one_block[:, :size]], axis=1)
            two_turned = jnp.concatenate([two_block[:, size:], two_block[:, :size]], axis=1)
            stacked.append(jnp.concatenate(
                [jnp.where(near, one_block, two_turned), jnp.where(near, one_turned, two_block)], axis=0
            ))
        stacked = jnp.concatenate(stacked, axis=1)
        made = [jnp.dot(expand_ref[rows[block]], stacked, preferred_element_type=F32) for block in (first, second)]
        for part, out_ref in enumerate(out_refs[2 * late:2 * late + 2]):
            lanes = slice(part * wide, (part + 1) * wide)
            out_ref[index] = jnp.where(near_out, made[0][:, lanes], made[1][:, lanes]).astype(BF16)

    for late in range(2):
        def work(indices, _, late=late):
            for index in indices:
                one(late, index)

        in_chunks(chunks, list_ref[2 * total + late], work)


def in_chunks(chunks, count, work):
    start = 0
    for length in chunks:
        indices = range(start, start + length)
        if start:
            pl.when(count > 2 * start)(functools.partial(work, indices, False))
        else:
            work(indices, True)
        start += length


def add_chi(late, chunks, list_ref, slots, owners, own_ref, other_ref, virt_ref, total_ref):
    _, wide, _ = own_ref.shape
    size = wide // 2
    turns, places, tiles = virt_ref.shape[:3]
    groups_dev = 2 * tiles
    groups = total_ref.shape[1]
    all_turns = groups // (places * groups_dev)
    total_blocks = owners.shape[0]
    count = list_ref[2 * total_blocks + late]
    me = lax.axis_index("blk") ^ (places * all_turns // 2)
    low = lax.broadcasted_iota(jnp.int32, (size, wide), 1) < size
    low_row = lax.broadcasted_iota(jnp.int32, (16, wide), 1) < size
    group_range = lax.broadcasted_iota(jnp.int32, (16, groups), 1)

    core = lax.axis_index("aux")

    def virt_of(place, slot, part):
        found = virt_ref[place & (turns - 1), place >> bits_of(all_turns), slot & (tiles - 1)]
        turned = jnp.concatenate([found[:, size:], found[:, :size]], axis=1)
        placed = jnp.where((slot // tiles) ^ core == part, found, turned)
        return jnp.where(low if part == 0 else ~low, placed, jnp.zeros_like(placed))

    def one(index, total):
        blocks = [list_ref[late * total_blocks + 2 * index + part] for part in range(2)]
        found = [(owners[block] ^ me) & (places * all_turns - 1) for block in blocks]
        columns = [place * groups_dev + slots[block] for place, block in zip(found, blocks)]
        virt = jnp.concatenate([virt_of(place, slots[block], part) for part, (place, block) in enumerate(zip(found, blocks))], axis=0)
        full = []
        for ref in (own_ref, other_ref):
            made = jnp.dot(ref[index], virt, preferred_element_type=F32).astype(BF16).astype(F32)
            full += [made[:size], made[size:]]
        sums = {}
        for p in range(4):
            for q in range(p, 4):
                sums[p, q] = sums[q, p] = jnp.sum(full[p] * full[q], axis=0, keepdims=True)
        rows = [sums[p, q] for p in range(2) for q in range(4)]
        rows += [sums[p, q ^ 2] for p in range(2, 4) for q in range(4)]
        values = jnp.concatenate(rows, axis=0)
        for part, where in enumerate((low_row, ~low_row)):
            column = jnp.where(2 * index + part < count, columns[part], -1)
            value = jnp.sum(jnp.where(where, values, 0.0), axis=1, keepdims=True)
            total = total + jnp.where(group_range == column, value, 0.0)
        return total

    def work(indices, is_first):
        total = jnp.zeros((16, groups), F32)
        for index in indices:
            total = one(index, total)
        total_ref[...] = total if is_first and not late else total_ref[...] + total

    in_chunks(chunks, count, work)


def early_kernel(chunks, list_ref, slots, owners, own_ref, other_ref, virt_ref, total_ref):
    add_chi(0, chunks, list_ref, slots, owners, own_ref, other_ref, virt_ref, total_ref)


def late_kernel(scale, chunks, list_ref, slots, owners, own_ref, other_ref, virt_ref, early_ref, out_ref, total_ref):
    total_ref[...] = early_ref[...]
    add_chi(1, chunks, list_ref, slots, owners, own_ref, other_ref, virt_ref, total_ref)
    summed = total_ref[...] * scale
    groups_dev = 2 * virt_ref.shape[2]
    places = summed.shape[1] // groups_dev
    rows = 8 * groups_dev
    lane = lax.broadcasted_iota(jnp.int32, (8, 2 * rows), 1) // groups_dev % 8
    sublane = lax.broadcasted_iota(jnp.int32, (8, 2 * rows), 0)
    quarter = places // 2
    core = lax.axis_index("aux")
    me = lax.axis_index("blk")
    out_ref[...] = jnp.zeros(out_ref.shape, F32)
    for target in range(2):
        wanted = jnp.where(core == target, summed[:8], summed[8:])
        if target:
            wanted = jnp.concatenate([wanted[2:4], wanted[:2], wanted[6:], wanted[4:6]], axis=0)
        for start in range(0, places, 8):
            piece = wanted[:, start * groups_dev:(start + 8) * groups_dev]
            piece = jnp.concatenate([piece, piece], axis=1)
            turned = jnp.zeros_like(piece)
            for shift in range(8):
                moved = pltpu.roll(pltpu.roll(piece, shift, 0), (2 * rows - groups_dev * shift) % (2 * rows), 1)
                turned = jnp.where(lane == (sublane + 8 - shift) % 8, moved, turned)
            for index in range(8):
                place = start + index
                second = place // quarter
                far = 2 * core + 1 - second
                owner = me ^ (far * quarter + place % quarter)
                out_ref[pl.ds(2 * owner + target, 1), :] = turned[index:index + 1, :rows]


def body(count, three_centre, occupied_blocks, virtual_blocks, row_slot, col_slot, block_owner):
    block_count, aux_local, width = three_centre.shape
    groups_dev, size, _ = occupied_blocks.shape
    scale = 0.25 / (size * size)
    wide = 2 * size
    pairs = block_count // 4
    core = lax.axis_index("aux")
    rounds = rounds_of(count)
    near, mid, far = rounds[0]

    def by_mu(values):
        found = values.reshape(block_count, aux_local, width // wide, wide)
        return found.transpose(0, 2, 1, 3).reshape(block_count, size, wide)

    def in_hbm(values):
        return pltpu.with_memory_space_constraint(values, pltpu.HBM)

    chunks = (5 * pairs // 8,) + (pairs // 8,) * 3 + (pairs // 4,) * 4
    tiles = groups_dev // 2
    virt = jnp.concatenate([lax.dynamic_slice_in_dim(virtual_blocks, core * tiles, tiles), lax.dynamic_slice_in_dim(virtual_blocks, (1 - core) * tiles, tiles)], axis=2)
    other = swap_cores(by_mu(three_centre))
    arrived = [split_flip(virt, near, far, count), split_flip(virt, 0, mid, count)]
    integers = pltpu.SMEM((block_count,), jnp.int32)
    options = dict(
        compiler_params=pltpu.CompilerParams(vmem_limit_bytes=16 * 1024 * 1024),
        cost_estimate=pl.CostEstimate(flops=10**9, bytes_accessed=4 * 1024 * 1024, transcendentals=0),
    )
    all_turns = len(rounds[-1]) + 1
    expanded, block_list, rows, slots, owners = pl.pallas_call(
        functools.partial(ready_kernel, count, bits_of(all_turns) - 1),
        out_shape=[
            jax.ShapeDtypeStruct((groups_dev, wide, wide), BF16),
            pltpu.SMEM((2 * block_count + 2,), jnp.int32),
            integers,
            integers,
            integers,
        ],
        in_specs=[HBM] * 4,
        out_specs=[VMEM] + [SMEM] * 4,
        scratch_shapes=[pltpu.VMEM((groups_dev, size, size), BF16), pltpu.SemaphoreType.DMA((4,))],
        name="ready",
        **options,
    )(in_hbm(row_slot), in_hbm(col_slot), in_hbm(block_owner.reshape(block_count)), in_hbm(occupied_blocks))
    arrived, expanded = lax.optimization_barrier((arrived, expanded))
    virt = jnp.stack(arrived)
    half_shape = jax.ShapeDtypeStruct((2 * pairs, wide, wide), BF16)
    halves = pl.pallas_call(
        functools.partial(half_kernel, chunks),
        out_shape=[half_shape] * 4,
        in_specs=[SMEM] * 2 + [VMEM] * 3,
        out_specs=[VMEM] * 4,
        name="half",
        **options,
    )(block_list, rows, by_mu(three_centre), other, expanded)
    for distances in rounds[1:-1]:
        arrived = [flip(virt, distance, count) for distance in distances]
        virt = jnp.stack([virt] + arrived, axis=1).reshape((-1,) + virt.shape[1:])
    arrived = [virt] + [flip(virt, distance, count) for distance in rounds[-1]]
    arrived[:2], halves = lax.optimization_barrier((arrived[:2], halves))
    early = jnp.stack(arrived[:all_turns // 2])
    places = count // 2
    total_shape = (16, places * groups_dev)
    total = pl.pallas_call(
        functools.partial(early_kernel, chunks),
        out_shape=jax.ShapeDtypeStruct(total_shape, F32),
        in_specs=[SMEM] * 3 + [VMEM] * 3,
        out_specs=VMEM,
        name="early",
        **options,
    )(block_list, slots, owners, *halves[:2], early)
    arrived, total = lax.optimization_barrier((arrived[all_turns // 2:], total))
    partial = pl.pallas_call(
        functools.partial(late_kernel, scale, chunks),
        out_shape=jax.ShapeDtypeStruct((2 * count, 8 * groups_dev), F32),
        in_specs=[SMEM] * 3 + [VMEM] * 4,
        out_specs=VMEM,
        scratch_shapes=[pltpu.VMEM(total_shape, F32)],
        name="late",
        **options,
    )(block_list, slots, owners, *halves[2:], jnp.stack(arrived), total)

    arrived = lax.all_to_all(partial, ("blk", "aux"), 0, 0, tiled=True)
    return jnp.sum(arrived, axis=0).reshape(2, 4, groups_dev).transpose(2, 0, 1)


def solution(mesh):
    in_specs = (
        P("blk", "aux", None),
        P("blk", None, None),
        P("blk", None, None),
        P("blk"),
        P("blk"),
        P("blk", None),
    )
    out_specs = P("blk", "aux", None)
    return jax.shard_map(
        functools.partial(body, mesh.shape["blk"]),
        mesh=mesh,
        in_specs=in_specs,
        out_specs=out_specs,
        check_vma=False,
    )
```

```python
import functools

import jax
import jax.numpy as jnp
from jax import lax
from jax.experimental import pallas as pl
from jax.experimental.pallas import tpu as pltpu
from jax.sharding import PartitionSpec as P

F32 = jnp.float32
BF16 = jnp.bfloat16
SMEM = pl.BlockSpec(memory_space=pltpu.SMEM)
VMEM = pl.BlockSpec(memory_space=pltpu.VMEM)
HBM = pl.BlockSpec(memory_space=pltpu.HBM)


def rounds_of(count):
    bits = count.bit_length() - 1
    found = []
    while bits:
        low = max(bits - 2, 0)
        found.append([step << low for step in range(1, 1 << (bits - low))])
        bits = low
    return found


def flip(values, distance, count):
    return lax.ppermute(values, "blk", [(i, i ^ distance) for i in range(count)])


def swap_cores(values):
    return lax.ppermute(values, "aux", [(0, 1), (1, 0)])


def split_flip(values, core_zero, core_one, count):
    pairs = [(2 * i + core, 2 * (i ^ distance) + core) for i in range(count) for core, distance in enumerate((core_zero, core_one))]
    return lax.ppermute(values, ("blk", "aux"), pairs)


def expand(occ_ref, expand_ref):
    groups, size, _ = occ_ref.shape
    wide = 2 * size
    column = lax.broadcasted_iota(jnp.int32, (size, wide), 1)
    mu = lax.broadcasted_iota(jnp.int32, (size, wide), 0)
    order = jnp.where(mu == (column % size) // 2 * 2 + column // size, 1.0, 0.0).astype(BF16)
    left = lax.broadcasted_iota(jnp.int32, (wide, wide), 0) // size
    same = left == lax.broadcasted_iota(jnp.int32, (wide, wide), 1) % 2
    for group in range(groups):
        occ = occ_ref[group]
        twice = jnp.concatenate([occ, occ], axis=1)
        spread = lax.dot_general(twice, order, (((0,), (0,)), ((), ())), preferred_element_type=F32)
        expand_ref[group] = jnp.where(same, spread, 0.0).astype(BF16)


def bits_of(size):
    return size.bit_length() - 1


def list_blocks(count, late_bit, owners, list_ref):
    total = owners.shape[0]
    quarter = count // 4
    core = lax.axis_index("aux")
    me = lax.axis_index("blk") ^ quarter

    def add(block, found):
        early, late = found
        away = owners[block] ^ me
        mine = (away >> (bits_of(quarter) + 1)) ^ (1 - core)
        late_here = mine & (away >> late_bit)
        list_ref[jnp.where((away >> late_bit) & 1 == 1, late, early)] = block
        return early + mine - late_here, late + late_here

    early, late = lax.fori_loop(0, total, add, (jnp.int32(0), jnp.int32(total)), unroll=8)
    list_ref[2 * total] = early
    list_ref[2 * total + 1] = late - total


def ready_kernel(
    count, late_bit, rows_ref, slots_ref, owners_ref, occ_ref, expand_ref, list_ref, rows, slots, owners, occ, sems
):
    copies = [
        pltpu.make_async_copy(source, target, sems.at[index])
        for index, (source, target) in enumerate(
            [(owners_ref, owners), (slots_ref, slots), (rows_ref, rows), (occ_ref, occ)]
        )
    ]
    for copy in copies:
        copy.start()

    def clear(index, _):
        list_ref[index] = 0
        return 0

    lax.fori_loop(0, list_ref.shape[0], clear, 0, unroll=43)
    copies[0].wait()
    list_blocks(count, late_bit, owners, list_ref)
    copies[3].wait()
    expand(occ, expand_ref)
    copies[1].wait()
    copies[2].wait()


def half_kernel(chunks, list_ref, rows, own_ref, other_ref, expand_ref, *out_refs):
    total = own_ref.shape[0]
    wide = expand_ref.shape[1]
    size = wide // 2
    near = lax.broadcasted_iota(jnp.int32, (size, wide), 1) < size
    near_out = lax.broadcasted_iota(jnp.int32, (wide, wide), 1) < size

    def one(late, index):
        first, second = [list_ref[late * total + 2 * index + part] for part in range(2)]
        stacked = []
        for source in (own_ref, other_ref):
            one_block, two_block = source[first], source[second]
            one_turned = jnp.concatenate([one_block[:, size:], one_block[:, :size]], axis=1)
            two_turned = jnp.concatenate([two_block[:, size:], two_block[:, :size]], axis=1)
            stacked.append(jnp.concatenate(
                [jnp.where(near, one_block, two_turned), jnp.where(near, one_turned, two_block)], axis=0
            ))
        stacked = jnp.concatenate(stacked, axis=1)
        made = [jnp.dot(expand_ref[rows[block]], stacked, preferred_element_type=F32) for block in (first, second)]
        for part, out_ref in enumerate(out_refs[2 * late:2 * late + 2]):
            lanes = slice(part * wide, (part + 1) * wide)
            out_ref[index] = jnp.where(near_out, made[0][:, lanes], made[1][:, lanes]).astype(BF16)

    for late in range(2):
        def work(indices, _, late=late):
            for index in indices:
                one(late, index)

        in_chunks(chunks, list_ref[2 * total + late], work)


def in_chunks(chunks, count, work):
    start = 0
    for length in chunks:
        indices = range(start, start + length)
        if start:
            pl.when(count > 2 * start)(functools.partial(work, indices, False))
        else:
            work(indices, True)
        start += length


def add_chi(late, chunks, list_ref, slots, owners, own_ref, other_ref, virt_ref, total_ref):
    _, wide, _ = own_ref.shape
    size = wide // 2
    turns, places, tiles = virt_ref.shape[:3]
    groups_dev = 2 * tiles
    groups = total_ref.shape[1]
    all_turns = groups // (places * groups_dev)
    total_blocks = owners.shape[0]
    count = list_ref[2 * total_blocks + late]
    me = lax.axis_index("blk") ^ (places * all_turns // 2)
    low = lax.broadcasted_iota(jnp.int32, (size, wide), 1) < size
    low_row = lax.broadcasted_iota(jnp.int32, (16, wide), 1) < size
    group_range = lax.broadcasted_iota(jnp.int32, (16, groups), 1)

    def virt_of(place, slot, part):
        found = virt_ref[place & (turns - 1), place >> bits_of(all_turns), slot & (tiles - 1)]
        turned = jnp.concatenate([found[:, size:], found[:, :size]], axis=1)
        placed = jnp.where(slot // tiles == part, found, turned)
        return jnp.where(low if part == 0 else ~low, placed, jnp.zeros_like(placed))

    def one(index, total):
        blocks = [list_ref[late * total_blocks + 2 * index + part] for part in range(2)]
        found = [(owners[block] ^ me) & (places * all_turns - 1) for block in blocks]
        columns = [place * groups_dev + slots[block] for place, block in zip(found, blocks)]
        virt = jnp.concatenate([virt_of(place, slots[block], part) for part, (place, block) in enumerate(zip(found, blocks))], axis=0)
        full = []
        for ref in (own_ref, other_ref):
            made = jnp.dot(ref[index], virt, preferred_element_type=F32).astype(BF16).astype(F32)
            full += [made[:size], made[size:]]
        sums = {}
        for p in range(4):
            for q in range(p, 4):
                sums[p, q] = sums[q, p] = jnp.sum(full[p] * full[q], axis=0, keepdims=True)
        rows = [sums[p, q] for p in range(2) for q in range(4)]
        rows += [sums[p, q ^ 2] for p in range(2, 4) for q in range(4)]
        values = jnp.concatenate(rows, axis=0)
        for part, where in enumerate((low_row, ~low_row)):
            column = jnp.where(2 * index + part < count, columns[part], -1)
            value = jnp.sum(jnp.where(where, values, 0.0), axis=1, keepdims=True)
            total = total + jnp.where(group_range == column, value, 0.0)
        return total

    def work(indices, is_first):
        total = jnp.zeros((16, groups), F32)
        for index in indices:
            total = one(index, total)
        total_ref[...] = total if is_first and not late else total_ref[...] + total

    in_chunks(chunks, count, work)


def early_kernel(chunks, list_ref, slots, owners, own_ref, other_ref, virt_ref, total_ref):
    add_chi(0, chunks, list_ref, slots, owners, own_ref, other_ref, virt_ref, total_ref)


def late_kernel(scale, chunks, list_ref, slots, owners, own_ref, other_ref, virt_ref, early_ref, out_ref, total_ref):
    total_ref[...] = early_ref[...]
    add_chi(1, chunks, list_ref, slots, owners, own_ref, other_ref, virt_ref, total_ref)
    summed = total_ref[...] * scale
    groups_dev = 2 * virt_ref.shape[2]
    places = summed.shape[1] // groups_dev
    rows = 8 * groups_dev
    lane = lax.broadcasted_iota(jnp.int32, (8, 2 * rows), 1) // groups_dev % 8
    sublane = lax.broadcasted_iota(jnp.int32, (8, 2 * rows), 0)
    quarter = places // 2
    core = lax.axis_index("aux")
    me = lax.axis_index("blk")
    out_ref[...] = jnp.zeros(out_ref.shape, F32)
    for target in range(2):
        wanted = jnp.where(core == target, summed[:8], summed[8:])
        if target:
            wanted = jnp.concatenate([wanted[2:4], wanted[:2], wanted[6:], wanted[4:6]], axis=0)
        for start in range(0, places, 8):
            piece = wanted[:, start * groups_dev:(start + 8) * groups_dev]
            piece = jnp.concatenate([piece, piece], axis=1)
            turned = jnp.zeros_like(piece)
            for shift in range(8):
                moved = pltpu.roll(pltpu.roll(piece, shift, 0), (2 * rows - groups_dev * shift) % (2 * rows), 1)
                turned = jnp.where(lane == (sublane + 8 - shift) % 8, moved, turned)
            for index in range(8):
                place = start + index
                second = place // quarter
                far = 2 * core + 1 - second
                owner = me ^ (far * quarter + place % quarter)
                out_ref[pl.ds(2 * owner + target, 1), :] = turned[index:index + 1, :rows]


def body(count, three_centre, occupied_blocks, virtual_blocks, row_slot, col_slot, block_owner):
    block_count, aux_local, width = three_centre.shape
    groups_dev, size, _ = occupied_blocks.shape
    scale = 0.25 / (size * size)
    wide = 2 * size
    pairs = block_count // 4
    core = lax.axis_index("aux")
    rounds = rounds_of(count)
    near, mid, far = rounds[0]

    def by_mu(values):
        found = values.reshape(block_count, aux_local, width // wide, wide)
        return found.transpose(0, 2, 1, 3).reshape(block_count, size, wide)

    def in_hbm(values):
        return pltpu.with_memory_space_constraint(values, pltpu.HBM)

    chunks = (5 * pairs // 8,) + (pairs // 8,) * 3 + (pairs // 4,) * 4
    tiles = groups_dev // 2
    virt = jnp.concatenate([virtual_blocks[:tiles], virtual_blocks[tiles:]], axis=2)
    other = swap_cores(by_mu(three_centre))
    arrived = [split_flip(virt, near, far, count), split_flip(virt, 0, mid, count)]
    integers = pltpu.SMEM((block_count,), jnp.int32)
    options = dict(
        compiler_params=pltpu.CompilerParams(vmem_limit_bytes=16 * 1024 * 1024),
        cost_estimate=pl.CostEstimate(flops=10**9, bytes_accessed=4 * 1024 * 1024, transcendentals=0),
    )
    all_turns = len(rounds[-1]) + 1
    expanded, block_list, rows, slots, owners = pl.pallas_call(
        functools.partial(ready_kernel, count, bits_of(all_turns) - 1),
        out_shape=[
            jax.ShapeDtypeStruct((groups_dev, wide, wide), BF16),
            pltpu.SMEM((2 * block_count + 2,), jnp.int32),
            integers,
            integers,
            integers,
        ],
        in_specs=[HBM] * 4,
        out_specs=[VMEM] + [SMEM] * 4,
        scratch_shapes=[pltpu.VMEM((groups_dev, size, size), BF16), pltpu.SemaphoreType.DMA((4,))],
        name="ready",
        **options,
    )(in_hbm(row_slot), in_hbm(col_slot), in_hbm(block_owner.reshape(block_count)), in_hbm(occupied_blocks))
    arrived, expanded = lax.optimization_barrier((arrived, expanded))
    virt = jnp.stack(arrived)
    half_shape = jax.ShapeDtypeStruct((2 * pairs, wide, wide), BF16)
    halves = pl.pallas_call(
        functools.partial(half_kernel, chunks),
        out_shape=[half_shape] * 4,
        in_specs=[SMEM] * 2 + [VMEM] * 3,
        out_specs=[VMEM] * 4,
        name="half",
        **options,
    )(block_list, rows, by_mu(three_centre), other, expanded)
    for distances in rounds[1:-1]:
        arrived = [flip(virt, distance, count) for distance in distances]
        virt = jnp.stack([virt] + arrived, axis=1).reshape((-1,) + virt.shape[1:])
    arrived = [virt] + [flip(virt, distance, count) for distance in rounds[-1]]
    arrived[:2], halves = lax.optimization_barrier((arrived[:2], halves))
    early = jnp.stack(arrived[:all_turns // 2])
    places = count // 2
    total_shape = (16, places * groups_dev)
    total = pl.pallas_call(
        functools.partial(early_kernel, chunks),
        out_shape=jax.ShapeDtypeStruct(total_shape, F32),
        in_specs=[SMEM] * 3 + [VMEM] * 3,
        out_specs=VMEM,
        name="early",
        **options,
    )(block_list, slots, owners, *halves[:2], early)
    arrived, total = lax.optimization_barrier((arrived[all_turns // 2:], total))
    partial = pl.pallas_call(
        functools.partial(late_kernel, scale, chunks),
        out_shape=jax.ShapeDtypeStruct((2 * count, 8 * groups_dev), F32),
        in_specs=[SMEM] * 3 + [VMEM] * 4,
        out_specs=VMEM,
        scratch_shapes=[pltpu.VMEM(total_shape, F32)],
        name="late",
        **options,
    )(block_list, slots, owners, *halves[2:], jnp.stack(arrived), total)

    arrived = lax.all_to_all(partial, ("blk", "aux"), 0, 0, tiled=True)
    return jnp.sum(arrived, axis=0).reshape(2, 4, groups_dev).transpose(2, 0, 1)


def solution(mesh):
    in_specs = (
        P("blk", "aux", None),
        P("blk", None, None),
        P("blk", None, None),
        P("blk"),
        P("blk"),
        P("blk", None),
    )
    out_specs = P("blk", "aux", None)
    return jax.shard_map(
        functools.partial(body, mesh.shape["blk"]),
        mesh=mesh,
        in_specs=in_specs,
        out_specs=out_specs,
        check_vma=False,
    )
```
